1024 devices in a mesh: dp: 16 (over x, core), node: 8 (over z), local: 8 (over y).
Axes of the slice: x: 8, y: 8, z: 8, core: 2. Of those that a mesh axis runs over, the one named last changes fastest.
Arguments:
- tokens: bfloat16 [3072, 4096], P(('node', 'local'), 'dp'), may hold values from -6 to 6
- cotangent: bfloat16 [3072, 4096], P(('node', 'local'), 'dp'), may hold values from -0.59765625 to 0.59765625
- routes: int32 [3072, 8], P(('node', 'local')), may hold values from 0 to 127, as said below
- gate_weights: float32 [3072, 8], P(('node', 'local')), may hold values from 0.1 to 0.6
- w_gate: bfloat16 [128, 4096, 1024], P(('node', 'local'), 'dp'), may hold values from -0.09375 to 0.09375
- w_up: bfloat16 [128, 4096, 1024], P(('node', 'local'), 'dp'), may hold values from -0.09375 to 0.09375
- w_down: bfloat16 [128, 1024, 4096], P(('node', 'local'), None, 'dp'), may hold values from -0.1875 to 0.1875
Outputs:
- mixed_out: bfloat16 [3072, 4096], P(('node', 'local'), 'dp')
- grad_tokens: bfloat16 [3072, 4096], P(('node', 'local'), 'dp')
- grad_gates: float32 [3072, 8], P(('node', 'local'))
The draws below stay inside these ranges and needn't reach their ends.
Inputs may be any that keep to these rules, and one draw needn't show every extreme that they name: `routes`: each row names 8 different experts, 2 from each of 4 node groups (expert e lies in group e // 16). In each aligned block of 48 rows one node group is named by every row, and no expert is named by more than 6 rows, some exactly 6.
All inputs are finite; a program needn't handle non-finite values.
Results may differ from the reference program's by a relative error of at most 0.005.
Values may be sent and summed in bfloat16 or wider, within the bound.
A program may use at most 32 MiB of HBM per device.

```python
import jax
import jax.numpy as jnp
from jax import lax

D = 4096
H = 1024
TOP = 8
TOK_DEV = 48
PEERS = 64
EXPERTS = 128
GROUP = 16
LIMIT = 4
PICKS = 2
CAP = 6
SLOTS = 384
TOKENS = 3072
N_NODE = 8


def draw_routes(key, part):
    key = jax.random.fold_in(key, 11)
    key_hot, key_pick, key_order, key_shuffle = jax.random.split(key, 4)
    hot_group = jax.random.randint(key_hot, (PEERS, 1, 1), 0, N_NODE)
    group_iota = lax.broadcasted_iota(jnp.int32, (PEERS, TOK_DEV, N_NODE), 2)
    scores = jax.random.randint(key_pick, (PEERS, TOK_DEV, N_NODE), 0, 1 << 20) * N_NODE + group_iota
    scores = jnp.where(group_iota == hot_group, -1, scores)
    unused, others = lax.top_k(scores, LIMIT - 1)
    chosen = jnp.concatenate([jnp.broadcast_to(hot_group, (PEERS, TOK_DEV, 1)), others.astype(jnp.int32)], axis=2)
    member = jnp.sum((chosen[:, :, :, None] == group_iota[:, :, None, :]).astype(jnp.int32), axis=2)
    rank_all = jnp.cumsum(member, axis=1) - member
    rank_sel = jnp.take_along_axis(rank_all, chosen, axis=2)
    order_scores = jax.random.randint(key_order, (PEERS, N_NODE, GROUP), 0, 1 << 20) * GROUP + lax.broadcasted_iota(jnp.int32, (PEERS, N_NODE, GROUP), 2)
    order = jnp.argsort(order_scores, axis=2).astype(jnp.int32)
    order_wide = jnp.broadcast_to(order[:, None, :, :], (PEERS, TOK_DEV, N_NODE, GROUP))
    chosen_wide = jnp.broadcast_to(chosen[:, :, :, None], (PEERS, TOK_DEV, LIMIT, GROUP))
    group_order = jnp.take_along_axis(order_wide, chosen_wide, axis=2)
    stepping = lax.broadcasted_iota(jnp.int32, (PEERS, TOK_DEV, LIMIT, PICKS), 3)
    within = (rank_sel[:, :, :, None] * PICKS + stepping) % GROUP
    local_pick = jnp.take_along_axis(group_order, within, axis=3)
    experts_named = (chosen[:, :, :, None] * GROUP + local_pick).reshape(TOKENS, TOP)
    shuffle_scores = jax.random.randint(key_shuffle, (TOKENS, TOP), 0, 1 << 20) * TOP + lax.broadcasted_iota(jnp.int32, (TOKENS, TOP), 1)
    shuffle = jnp.argsort(shuffle_scores, axis=1).astype(jnp.int32)
    return jnp.take_along_axis(experts_named, shuffle, axis=1).astype(jnp.int32)


def level_of(rng, shape, cuts, smallest, high):
    gain = 1.0
    for position, shards_of in cuts:
        steps = jax.random.uniform(jax.random.fold_in(jax.random.fold_in(rng, 6), position), (shards_of,), jnp.float32, smallest / len(cuts), high / len(cuts))
        gain = gain * jnp.repeat(jnp.exp(steps), shape[position] // shards_of).reshape((-1,) + (1,) * (len(shape) - 1 - position))
    return gain


def scatter_about(stream_key, shape, width, bound, cuts=(), held_as=jnp.bfloat16):
    drawn = jax.random.normal(stream_key, shape, jnp.float32) * width
    if len(cuts) > 0:
        drawn = level_of(stream_key, shape, cuts, -0.22, 0.18) * drawn
    return jnp.clip(drawn, min=-bound, max=bound).astype(held_as)


def setup_inputs(seed: int = 0) -> dict:
    arg_keys = jax.random.split(jax.random.key(seed), 8)
    return {
        "tokens": scatter_about(arg_keys[0], (TOKENS, D), 1.0, 6.0, ((0, 64), (1, 16))),
        "cotangent": scatter_about(arg_keys[1], (TOKENS, D), 0.1, 0.59765625, ((0, 64), (1, 16))),
        "routes": draw_routes(jax.random.fold_in(arg_keys[7], 71), 0),
        "gate_weights": jnp.clip(0.1 + 0.5 * jax.random.uniform(arg_keys[3], (TOKENS, TOP), jnp.float32) ** level_of(arg_keys[3], (TOKENS, TOP), ((0, 64),), -0.2, 0.2), 0.1, 0.6),
        "w_gate": scatter_about(arg_keys[4], (EXPERTS, D, H), D ** -0.5, 0.09375, ((0, 64), (1, 16))),
        "w_up": scatter_about(arg_keys[5], (EXPERTS, D, H), D ** -0.5, 0.09375, ((0, 64), (1, 16))),
        "w_down": scatter_about(arg_keys[6], (EXPERTS, H, D), H ** -0.5, 0.1875, ((0, 64), (2, 16))),
    }


BALANCE = 2.0


def slot_ranks(routes):
    onehot = (routes[:, :, None] == jnp.arange(EXPERTS, dtype=jnp.int32)[None, None, :]).astype(jnp.int32)
    present = jnp.sum(onehot, axis=1).reshape(TOKENS // TOK_DEV, TOK_DEV, EXPERTS)
    before = (jnp.cumsum(present, axis=1) - present).reshape(TOKENS, EXPERTS)
    slot_rank = jnp.sum(onehot * before[:, None, :], axis=2).astype(jnp.int32)
    return onehot, slot_rank


def reference(tokens, cotangent, routes, gate_weights, w_gate, w_up, w_down):
    onehot, slot_rank = slot_ranks(routes)
    owner_dev = (jnp.arange(TOKENS, dtype=jnp.int32) // TOK_DEV)[:, None]
    column = (owner_dev * CAP + slot_rank).astype(jnp.int32)
    token_ids = jnp.broadcast_to(jnp.arange(TOKENS, dtype=jnp.int32)[:, None], (TOKENS, TOP))
    slot_table = jnp.full((EXPERTS, SLOTS), TOKENS, jnp.int32).at[routes, column].set(token_ids)
    padded_tokens = jnp.concatenate([tokens, jnp.zeros((1, D), tokens.dtype)], axis=0)
    padded_grads = jnp.concatenate([cotangent, jnp.zeros((1, D), cotangent.dtype)], axis=0)

    def expert(pieces):
        gate_w, up_w, down_w, slot_rows = pieces
        token_rows = padded_tokens[slot_rows]
        grad_rows = padded_grads[slot_rows]
        gate_sum = jnp.dot(token_rows, gate_w, preferred_element_type=jnp.float32)
        up_sum = jnp.dot(token_rows, up_w, preferred_element_type=jnp.float32)
        back_sum = jnp.dot(grad_rows, down_w.T, preferred_element_type=jnp.float32)
        logistic = jax.nn.sigmoid(gate_sum)
        active = gate_sum * logistic
        hidden = (active * up_sum).astype(jnp.bfloat16)
        d_gate = (back_sum * up_sum * logistic * (1.0 + gate_sum * (1.0 - logistic))).astype(jnp.bfloat16)
        d_up = (back_sum * active).astype(jnp.bfloat16)
        forward_rows = jnp.dot(hidden, down_w, preferred_element_type=jnp.float32)
        input_rows = jnp.dot(d_gate, gate_w.T, preferred_element_type=jnp.float32) + jnp.dot(d_up, up_w.T, preferred_element_type=jnp.float32)
        return forward_rows, input_rows

    forward_all, input_all = lax.map(expert, (w_gate, w_up, w_down, slot_table))
    forward_rows = forward_all[routes, column]
    input_rows = input_all[routes, column]
    weights = gate_weights[:, :, None]
    mixed_out = jnp.sum(weights * forward_rows, axis=1).astype(jnp.bfloat16)
    grad_tokens = jnp.sum(weights * input_rows, axis=1).astype(jnp.bfloat16)
    inner_dot = jnp.sum(cotangent.astype(jnp.float32)[:, None, :] * forward_rows, axis=2)
    counts = jnp.sum(onehot, axis=(0, 1)).astype(jnp.float32)
    frequency = counts * EXPERTS / (TOP * TOKENS)
    grad_gates = inner_dot + BALANCE * frequency[routes]
    return mixed_out, grad_tokens, grad_gates
```

```python
import functools

import jax
import jax.numpy as jnp
from jax import lax
from jax.experimental import pallas as pl
from jax.experimental.pallas import tpu as pltpu
from jax.sharding import PartitionSpec as P

BALANCE = 2.0
CAP = 6
SUBS = 4
STEPS = 32766.0
MESH = pl.DeviceIdType.MESH
F32, BF16 = jnp.float32, jnp.bfloat16
VMEM = pl.BlockSpec(memory_space=pltpu.VMEM)
ANY = pl.BlockSpec(memory_space=pl.ANY)
LIMIT = 56 * 1024 * 1024


def greet(peers):
    barrier = pltpu.get_barrier_semaphore()
    for peer in peers:
        pl.semaphore_signal(barrier, inc=1, device_id=peer, device_id_type=MESH)
    pl.semaphore_wait(barrier, len(peers))


def push(src, dst, send, recv, peer):
    copy = pltpu.make_async_remote_copy(
        src_ref=src, dst_ref=dst, send_sem=send, recv_sem=recv, device_id=peer, device_id_type=MESH
    )
    copy.start()
    return copy


def other_core():
    core = lax.rem(lax.axis_index("dp"), 2)
    return core, lax.axis_index("dp") + 1 - 2 * core


def spread_kernel(nodes, tok, cot, meta, wg, wu, wd, tokz, cotz, metaz, wg2, wu2, wd2, send, recv, wsend, wrecv):
    me = lax.axis_index("node")
    core, twin = other_core()
    peers = [{"node": lax.rem(me + step, nodes)} for step in range(1, nodes)]
    greet(peers + [{"dp": twin}])
    copies = []
    for step in range(1, nodes):
        for index, (src, dst) in enumerate(((meta, metaz), (tok, tokz), (cot, cotz))):
            copies.append(push(src, dst.at[me], send.at[step - 1, index], recv.at[step - 1, index], peers[step - 1]))
    for index, (src, dst) in enumerate(((wg, wg2), (wu, wu2), (wd, wd2))):
        copies.append(push(src.at[1 - core], dst, wsend.at[index], wrecv.at[index], {"dp": twin}))
    tokz[me] = tok[...]
    cotz[me] = cot[...]
    metaz[me] = meta[...]
    for copy in copies:
        copy.wait()


def spread(nodes, tok, cot, meta, wg, wu, wd):
    arrays = (tok, cot, meta)
    weights = (wg, wu, wd)
    return pl.pallas_call(
        functools.partial(spread_kernel, nodes),
        out_shape=[jax.ShapeDtypeStruct((nodes,) + a.shape, a.dtype) for a in arrays]
        + [jax.ShapeDtypeStruct(a.shape[1:], a.dtype) for a in weights],
        in_specs=[VMEM] * 3 + [ANY] * 3,
        out_specs=[VMEM] * 3 + [ANY] * 3,
        scratch_shapes=[pltpu.SemaphoreType.DMA((nodes - 1, 3))] * 2 + [pltpu.SemaphoreType.DMA((3,))] * 2,
        compiler_params=pltpu.CompilerParams(collective_id=0, has_side_effects=True, vmem_limit_bytes=LIMIT),
    )(tok, cot, meta, wg, wu, wd)


def slot_codes(rows, experts, top, routes):
    columns = routes.shape[1]
    base = (lax.axis_index("node") * experts).astype(F32)
    name = lax.broadcasted_iota(jnp.int32, (experts, columns), 0).astype(F32) + base
    chosen = jnp.zeros((experts, columns), F32)
    for k in range(top):
        chosen = chosen + jnp.where(routes[k : k + 1, :] == name, 1.0, 0.0)
    scale = -(-32768 // rows)
    earlier = lax.broadcasted_iota(jnp.int32, (columns, columns), 0)
    later = lax.broadcasted_iota(jnp.int32, (columns, columns), 1)
    block_row = (earlier * scale) >> 15
    block_col = (later * scale) >> 15
    before = jnp.where((block_row == block_col) & (earlier < later), 1.0, 0.0).astype(BF16)
    rank = jnp.dot(chosen.astype(BF16), before, preferred_element_type=F32)
    block = (lax.broadcasted_iota(jnp.int32, (experts, columns), 1) * scale >> 15).astype(F32)
    code = jnp.where(chosen > 0.0, block * CAP + rank, -1.0)
    return name, chosen, code


def lay_out(metaz, top, rows):
    nodes = metaz.shape[0]
    weights = jnp.concatenate([metaz[i, :top, :rows] for i in range(nodes)], axis=1)
    routes = jnp.concatenate([metaz[i, top : 2 * top, :rows] for i in range(nodes)], axis=1)
    return weights, routes


def select_kernel(top, tokz, cotz, metaz, tok_out, cot_out, count_out):
    nodes, rows, features = tokz.shape
    experts, slots, _ = tok_out.shape
    _, routes = lay_out(metaz, top, rows)
    _, chosen, code = slot_codes(rows, experts, top, routes)
    columns = routes.shape[1]
    place = lax.broadcasted_iota(jnp.int32, (1, slots, 1), 1).astype(F32)
    pick = jnp.where(code[:, None, :] == place, 1.0, 0.0).astype(BF16).reshape(experts * slots, columns)
    for src, dst in ((tokz, tok_out), (cotz, cot_out)):
        got = jnp.dot(pick, src[...].reshape(columns, features), preferred_element_type=F32)
        dst[...] = got.astype(BF16).reshape(experts, slots, features)
    count_out[...] = jnp.broadcast_to(jnp.sum(chosen, axis=1, keepdims=True), count_out.shape)


def select(experts, top, tokz, cotz, metaz):
    nodes, rows, features = tokz.shape
    slots = nodes * CAP
    shape = jax.ShapeDtypeStruct((experts, slots, features), BF16)
    return pl.pallas_call(
        functools.partial(select_kernel, top),
        out_shape=[shape, shape, jax.ShapeDtypeStruct((experts, 128), F32)],
        in_specs=[VMEM] * 3,
        out_specs=[VMEM] * 3,
        compiler_params=pltpu.CompilerParams(vmem_limit_bytes=LIMIT),
    )(tokz, cotz, metaz)


def slots_kernel(locals_, tok, cot, count, tok_in, cot_in, count_sum, counts, send, recv, csend, crecv, near):
    me = lax.axis_index("local")
    core, twin = other_core()
    where = [lax.rem(me + step, locals_) for step in range(locals_)]
    same = [{"local": place} for place in where]
    cross = [{"local": place, "dp": twin} for place in where]
    greet(same[1:] + cross)
    copies = []
    for step in range(locals_):
        for far, peer in ((0, same[step]), (1, cross[step])):
            if step == 0 and far == 0:
                continue
            expert = 2 * where[step] + (core if far == 0 else 1 - core)
            for index, (src, dst) in enumerate(((tok, tok_in), (cot, cot_in))):
                at = (step, far, index)
                copies.append(push(src.at[expert], dst.at[far, me], send.at[at], recv.at[at], peer))
        if step > 0:
            copies.append(push(count, counts.at[me], csend.at[step - 1], crecv.at[step - 1], same[step]))
    mine = 2 * me + core
    own = []
    for index, (src, dst) in enumerate(((tok, tok_in), (cot, cot_in))):
        own.append(pltpu.make_async_copy(src.at[mine], dst.at[0, me], near.at[index]))
        own[-1].start()
    counts[me] = count[...]
    for copy in own + copies:
        copy.wait()
    count_sum[...] = jnp.sum(counts[...], axis=0)


def slots_exchange(locals_, tok, cot, count):
    experts, slots, features = tok.shape
    shape = jax.ShapeDtypeStruct((2, locals_, slots, features), BF16)
    return pl.pallas_call(
        functools.partial(slots_kernel, locals_),
        out_shape=[shape, shape, jax.ShapeDtypeStruct(count.shape, F32)],
        in_specs=[VMEM] * 3,
        out_specs=[VMEM] * 3,
        scratch_shapes=[pltpu.VMEM((locals_,) + count.shape, F32)]
        + [pltpu.SemaphoreType.DMA((locals_, 2, 2))] * 2
        + [pltpu.SemaphoreType.DMA((max(locals_ - 1, 1),))] * 2
        + [pltpu.SemaphoreType.DMA((2,))],
        compiler_params=pltpu.CompilerParams(collective_id=1, has_side_effects=True, vmem_limit_bytes=LIMIT),
    )(tok, cot, count)


NT = (((1,), (1,)), ((), ()))


def first_kernel(chips, core, tok, cot, wg, wu, wd, wg2, wu2, wd2, out, table):
    width = wg.shape[2]

    @pl.when(pl.program_id(0) == 0)
    def _():
        table[...] = jnp.zeros_like(table)

    gate = jnp.dot(tok[0], wg[0], preferred_element_type=F32) + jnp.dot(tok[1], wg2[...], preferred_element_type=F32)
    up = jnp.dot(tok[0], wu[0], preferred_element_type=F32) + jnp.dot(tok[1], wu2[...], preferred_element_type=F32)
    back = lax.dot_general(cot[0], wd[0], NT, preferred_element_type=F32)
    back = back + lax.dot_general(cot[1], wd2[...], NT, preferred_element_type=F32)
    for index, value in enumerate((gate, up, back)):
        out[0, :, index * width : (index + 1) * width] = value
        top = jnp.max(jnp.abs(value).reshape(chips, -1, width), axis=1)
        table[index] = jnp.maximum(table[index], jnp.max(top, axis=1, keepdims=True))


def first(chips, core, tok, cot, wg, wu, wd, wg2, wu2, wd2):
    _, rows, features = tok.shape
    hidden = wg.shape[2]
    width = hidden // SUBS
    whole = pl.BlockSpec((2, rows, features), lambda s, core: (0, 0, 0))
    return pl.pallas_call(
        functools.partial(first_kernel, chips),
        out_shape=[
            jax.ShapeDtypeStruct((SUBS, rows, 3 * width), F32),
            jax.ShapeDtypeStruct((3, chips, 128), F32),
        ],
        grid_spec=pltpu.PrefetchScalarGridSpec(
            num_scalar_prefetch=1,
            grid=(SUBS,),
            in_specs=[
                whole,
                whole,
                pl.BlockSpec((1, features, width), lambda s, core: (core[0], 0, s)),
                pl.BlockSpec((1, features, width), lambda s, core: (core[0], 0, s)),
                pl.BlockSpec((1, width, features), lambda s, core: (core[0], s, 0)),
                pl.BlockSpec((features, width), lambda s, core: (0, s)),
                pl.BlockSpec((features, width), lambda s, core: (0, s)),
                pl.BlockSpec((width, features), lambda s, core: (s, 0)),
            ],
            out_specs=[
                pl.BlockSpec((1, rows, 3 * width), lambda s, core: (s, 0, 0)),
                pl.BlockSpec((3, chips, 128), lambda s, core: (0, 0, 0)),
            ],
        ),
        compiler_params=pltpu.CompilerParams(vmem_limit_bytes=LIMIT),
    )(core, tok, cot, wg, wu, wd, wg2, wu2, wd2)


def ring_kernel(
    chips, part, table, shares, values, got, stage, bounds, bounds_in, rsend, rrecv, gsend, grecv, vsend, vrecv, tsend, trecv
):
    dp = lax.axis_index("dp")
    core = lax.rem(dp, 2)
    me = (dp - core) // 2
    depth = chips // 2
    half = SUBS // 2
    width = part.shape[3] // 3
    rows = part.shape[2]

    def chip(offset):
        return lax.rem(me + offset + 2 * chips, chips)

    way = [{"dp": 2 * chip(1) + core}, {"dp": 2 * chip(-1) + core}]
    sign = (1, -1)
    greet(way)

    def halves(direction):
        return range(half) if direction == 0 else range(half, SUBS)

    copies = []

    def bound(ref, chunk):
        lines = [jnp.broadcast_to(ref[index, pl.ds(chunk, 1), :], (1, 128)) for index in range(3)]
        return jnp.concatenate([line for line in lines for _ in range(width // 128)], axis=1)

    def reduce_send(direction, step, sub, total, chunk):
        at = (direction, step, sub)
        limit = bound(bounds.at[direction, step], chunk)
        inverse = jnp.where(limit > 1e-30, STEPS / jnp.maximum(limit, 1e-30), 0.0)
        stage[at] = jnp.round(total * inverse).astype(jnp.int32).astype(jnp.int16)
        copies.append(push(stage.at[at], got.at[at], rsend.at[at], rrecv.at[at], way[direction]))

    def reduce_wait(direction, step, sub, chunk):
        at = (direction, step, sub)
        pltpu.make_async_copy(got.at[at], got.at[at], rrecv.at[at]).wait()
        limit = bound(bounds_in.at[direction, step], chunk)
        return got[at].astype(jnp.int32).astype(F32) * (limit * (1.0 / STEPS))

    def bound_send(direction, step):
        at = (direction, step)
        copies.append(push(bounds.at[at], bounds_in.at[at], tsend.at[at], trecv.at[at], way[direction]))

    def bound_wait(direction, step):
        at = (direction, step)
        pltpu.make_async_copy(bounds_in.at[at], bounds_in.at[at], trecv.at[at]).wait()

    for direction in range(2):
        bounds[direction, 0] = table[...]
        bound_send(direction, 0)
    for index in range(half):
        for direction in range(2):
            sub = halves(direction)[index]
            chunk = chip(sign[direction] * depth)
            reduce_send(direction, 0, sub, part[sub, chunk], chunk)
    for step in range(1, depth):
        for direction in range(2):
            bound_wait(direction, step - 1)
            bounds[direction, step] = table[...] + bounds_in[direction, step - 1]
            bound_send(direction, step)
        for index in range(half):
            for direction in range(2):
                if step == 1:
                    sub = halves(1 - direction)[index]
                    chunk = chip(sign[direction] * (depth - 1))
                    reduce_send(direction, 1, sub, part[sub, chunk], chunk)
        for sub in range(SUBS):
            for direction in range(2):
                if step == 1 and sub not in halves(direction):
                    continue
                chunk = chip(sign[direction] * (depth - step))
                total = part[sub, chunk] + reduce_wait(direction, step - 1, sub, chunk)
                reduce_send(direction, step, sub, total, chunk)
    for direction in range(2):
        bound_wait(direction, depth - 1)

    def gather_send(direction, step, sub):
        chunk = shares.at[sub, chip(-sign[direction] * step)]
        at = (direction, step, sub)
        copies.append(push(chunk, chunk, gsend.at[at], grecv.at[at], way[direction]))

    def gather_wait(direction, step, sub):
        chunk = shares.at[sub, chip(-sign[direction] * (step + 1))]
        pltpu.make_async_copy(chunk, chunk, grecv.at[direction, step, sub]).wait()

    def value_send(direction, step):
        chunk = values.at[chip(-sign[direction] * step)]
        at = (direction, step)
        copies.append(push(chunk, chunk, vsend.at[at], vrecv.at[at], way[direction]))

    def value_wait(direction, step):
        chunk = values.at[chip(-sign[direction] * (step + 1))]
        pltpu.make_async_copy(chunk, chunk, vrecv.at[direction, step]).wait()

    inner = jnp.zeros((rows, 1), F32)
    for index in range(half):
        for sub in (halves(0)[index], halves(1)[index]):
            total = part[sub, me]
            for direction in range(2):
                if depth > 1 or sub in halves(direction):
                    total = total + reduce_wait(direction, depth - 1, sub, me)
            gate, up, back = total[:, :width], total[:, width : 2 * width], total[:, 2 * width :]
            logistic = 1.0 / (1.0 + jnp.exp(-gate))
            active = gate * logistic
            hidden = (active * up).astype(BF16)
            shares[sub, me, :, :width] = hidden
            d_gate = back * up * logistic * (1.0 + gate * (1.0 - logistic))
            shares[sub, me, :, width : 2 * width] = d_gate.astype(BF16)
            shares[sub, me, :, 2 * width :] = (back * active).astype(BF16)
            for direction in range(2):
                if depth > 1 or sub in halves(direction):
                    gather_send(direction, 0, sub)
            inner = inner + jnp.sum(hidden.astype(F32) * back, axis=1, keepdims=True)
    lanes = lax.broadcasted_iota(jnp.int32, (rows, 128), 1)
    diagonal = lax.broadcasted_iota(jnp.int32, (rows, 128), 0) == lanes
    line = jnp.sum(jnp.where(diagonal, inner, 0.0), axis=0, keepdims=True)
    values[me] = jnp.broadcast_to(line, (8, 128))
    for direction in range(2):
        if depth > 1 or direction == 0:
            value_send(direction, 0)
    for step in range(1, depth + 1):
        last = step == depth
        for index in range(half):
            for sub in (halves(0)[index], halves(1)[index]):
                for direction in range(2):
                    if last and sub not in halves(direction):
                        continue
                    gather_wait(direction, step - 1, sub)
                    if not last and (step < depth - 1 or sub in halves(direction)):
                        gather_send(direction, step, sub)
        for direction in range(2):
            if last and direction == 1:
                continue
            value_wait(direction, step - 1)
            if not last and (step < depth - 1 or direction == 0):
                value_send(direction, step)
    for copy in copies:
        copy.wait_send()


def ring(chips, part, table):
    _, _, rows, wide = part.shape
    depth = chips // 2
    return pl.pallas_call(
        functools.partial(ring_kernel, chips),
        out_shape=[jax.ShapeDtypeStruct(part.shape, BF16), jax.ShapeDtypeStruct((chips, 8, 128), F32)],
        in_specs=[VMEM] * 2,
        out_specs=[VMEM] * 2,
        scratch_shapes=[pltpu.VMEM((2, depth, SUBS, rows, wide), jnp.int16)] * 2
        + [pltpu.VMEM((2, depth) + table.shape, F32)] * 2
        + [pltpu.SemaphoreType.DMA((2, depth, SUBS))] * 4
        + [pltpu.SemaphoreType.DMA((2, depth))] * 4,
        compiler_params=pltpu.CompilerParams(collective_id=2, has_side_effects=True, vmem_limit_bytes=LIMIT),
    )(part, table)


def second_kernel(core, shares, wg, wu, wd, wg2, wu2, wd2, out):
    features = wg2.shape[0]
    width = wg2.shape[1] // SUBS
    for side, (gate, up, down) in enumerate(((wg.at[0], wu.at[0], wd.at[0]), (wg2, wu2, wd2))):
        forward = jnp.zeros(out.shape[1:2] + (features,), F32)
        back = forward
        for sub in range(SUBS):
            units = slice(sub * width, (sub + 1) * width)
            forward = forward + jnp.dot(shares[sub, :, :width], down[units, :], preferred_element_type=F32)
            back = back + lax.dot_general(
                shares[sub, :, width : 2 * width], gate[:, units], NT, preferred_element_type=F32
            )
            back = back + lax.dot_general(shares[sub, :, 2 * width :], up[:, units], NT, preferred_element_type=F32)
        out[side, :, :features] = forward.astype(BF16)
        out[side, :, features:] = back.astype(BF16)


def second(core, shares, wg, wu, wd, wg2, wu2, wd2):
    _, rows, wide = shares.shape
    features, hidden = wg2.shape
    side = pl.BlockSpec((features, hidden), lambda i, core: (0, 0))
    return pl.pallas_call(
        second_kernel,
        out_shape=jax.ShapeDtypeStruct((2, rows, 2 * features), BF16),
        grid_spec=pltpu.PrefetchScalarGridSpec(
            num_scalar_prefetch=1,
            grid=(1,),
            in_specs=[
                pl.BlockSpec((SUBS, rows, wide), lambda i, core: (0, 0, 0)),
                pl.BlockSpec((1, features, hidden), lambda i, core: (core[0], 0, 0)),
                pl.BlockSpec((1, features, hidden), lambda i, core: (core[0], 0, 0)),
                pl.BlockSpec((1, hidden, features), lambda i, core: (core[0], 0, 0)),
                side,
                side,
                pl.BlockSpec((hidden, features), lambda i, core: (0, 0)),
            ],
            out_specs=pl.BlockSpec((2, rows, 2 * features), lambda i, core: (0, 0, 0)),
        ),
        compiler_params=pltpu.CompilerParams(vmem_limit_bytes=LIMIT),
    )(core, shares, wg, wu, wd, wg2, wu2, wd2)


def return_kernel(locals_, rows, values, back, vback, send, recv, near):
    me = lax.axis_index("local")
    core, twin = other_core()
    where = [lax.rem(me + step, locals_) for step in range(locals_)]
    same = [{"local": place} for place in where]
    cross = [{"local": place, "dp": twin} for place in where]
    greet(same[1:] + cross)
    mine = 2 * me + core
    copies = []
    for step in range(locals_):
        for far, peer in ((0, same[step]), (1, cross[step])):
            if step == 0 and far == 0:
                continue
            at = (step, far)
            copies.append(push(rows.at[far, where[step]], back.at[mine], send.at[at + (0,)], recv.at[at + (0,)], peer))
            copies.append(push(values.at[where[step]], vback.at[mine], send.at[at + (1,)], recv.at[at + (1,)], peer))
    own = pltpu.make_async_copy(rows.at[0, me], back.at[mine], near)
    own.start()
    vback[mine] = values[me]
    own.wait()
    for copy in copies:
        copy.wait()


def give_back(locals_, rows, values):
    _, _, slots, wide = rows.shape
    return pl.pallas_call(
        functools.partial(return_kernel, locals_),
        out_shape=[
            jax.ShapeDtypeStruct((2 * locals_, slots, wide), BF16),
            jax.ShapeDtypeStruct((2 * locals_, 8, 128), F32),
        ],
        in_specs=[VMEM] * 2,
        out_specs=[VMEM] * 2,
        scratch_shapes=[pltpu.SemaphoreType.DMA((locals_, 2, 2))] * 2 + [pltpu.SemaphoreType.DMA],
        compiler_params=pltpu.CompilerParams(collective_id=3, has_side_effects=True, vmem_limit_bytes=LIMIT),
    )(rows, values)


def combine_kernel(top, scale, metaz, back, vback, count, out, gates_out):
    nodes = metaz.shape[0]
    experts, slots, wide = back.shape
    rows = out.shape[1]
    columns = nodes * rows
    weights, routes = lay_out(metaz, top, rows)
    name, _, code = slot_codes(rows, experts, top, routes)
    weight = jnp.zeros((experts, columns), F32)
    for k in range(top):
        weight = weight + jnp.where(routes[k : k + 1, :] == name, weights[k : k + 1, :], 0.0)
    place = lax.broadcasted_iota(jnp.int32, (1, slots, 1), 1).astype(F32)
    hit = code[:, None, :] == place
    rows_back = back[...].reshape(experts * slots, wide)
    high = weight.astype(BF16).astype(F32)
    total = jnp.zeros((columns, wide), F32)
    for share in (high, weight - high):
        spread_ = jnp.where(hit, share[:, None, :], 0.0).astype(BF16).reshape(experts * slots, columns)
        total = total + lax.dot_general(spread_, rows_back, (((0,), (0,)), ((), ())), preferred_element_type=F32)
    out[...] = total.astype(BF16).reshape(nodes, rows, wide)
    lanes = lax.broadcasted_iota(jnp.int32, (experts, slots, 128), 2)
    diagonal = lax.broadcasted_iota(jnp.int32, (experts, slots, 128), 1) == lanes
    value = jnp.sum(jnp.where(diagonal, vback[:, 0:1, :], 0.0), axis=2, keepdims=True)
    inner = jnp.sum(jnp.where(hit, value, 0.0), axis=1)
    inner = inner + BALANCE * scale * count[:, 0:1]
    gates = [
        jnp.sum(jnp.where(routes[k : k + 1, :] == name, inner, 0.0), axis=0, keepdims=True) for k in range(top)
    ]
    gates = jnp.concatenate(gates, axis=0)
    gates_out[...] = jnp.zeros_like(gates_out)
    for i in range(nodes):
        gates_out[i, :, :rows] = gates[:, i * rows : (i + 1) * rows]


def combine(top, scale, rows, metaz, back, vback, count):
    nodes = metaz.shape[0]
    return pl.pallas_call(
        functools.partial(combine_kernel, top, scale),
        out_shape=[
            jax.ShapeDtypeStruct((nodes, rows, back.shape[2]), BF16),
            jax.ShapeDtypeStruct((nodes, top, 128), F32),
        ],
        in_specs=[VMEM] * 4,
        out_specs=[VMEM] * 2,
        compiler_params=pltpu.CompilerParams(vmem_limit_bytes=LIMIT),
    )(metaz, back, vback, count)


def finish_kernel(nodes, rows, gates, mixed, grads, gates_out, got, got_gates, send, recv):
    me = lax.axis_index("node")
    where = [lax.rem(me + step, nodes) for step in range(nodes)]
    peers = [{"node": place} for place in where]
    greet(peers[1:])
    copies = []
    for step in range(1, nodes):
        for index, (src, dst) in enumerate(((rows, got), (gates, got_gates))):
            at = (step - 1, index)
            copies.append(push(src.at[where[step]], dst.at[step - 1], send.at[at], recv.at[at], peers[step]))
    for copy in copies:
        copy.wait()
    total = rows[me].astype(F32)
    gate = gates[me]
    for step in range(nodes - 1):
        total = total + got[step].astype(F32)
        gate = gate + got_gates[step]
    features = mixed.shape[1]
    mixed[...] = total[:, :features].astype(BF16)
    grads[...] = total[:, features:].astype(BF16)
    gates_out[...] = gate


def finish(rows, gates):
    nodes, count, wide = rows.shape
    half = jax.ShapeDtypeStruct((count, wide // 2), BF16)
    return pl.pallas_call(
        functools.partial(finish_kernel, nodes),
        out_shape=[half, half, jax.ShapeDtypeStruct(gates.shape[1:], F32)],
        in_specs=[VMEM] * 2,
        out_specs=[VMEM] * 3,
        scratch_shapes=[pltpu.VMEM((nodes - 1,) + rows.shape[1:], BF16), pltpu.VMEM((nodes - 1,) + gates.shape[1:], F32)]
        + [pltpu.SemaphoreType.DMA((nodes - 1, 2))] * 2,
        compiler_params=pltpu.CompilerParams(collective_id=4, has_side_effects=True, vmem_limit_bytes=LIMIT),
    )(rows, gates)


def body(chips, nodes, locals_, tokens, cotangent, routes, gate_weights, w_gate, w_up, w_down):
    rows, features = tokens.shape
    top = routes.shape[1]
    experts = 2 * locals_
    slots = nodes * CAP
    meta = jnp.concatenate([gate_weights.T, routes.T.astype(F32)], axis=0)
    meta = jnp.pad(meta, ((0, 0), (0, 128 - rows)))
    core = lax.rem(lax.axis_index("dp"), 2).astype(jnp.int32).reshape(1)
    tokz, cotz, metaz, *swapped = spread(nodes, tokens, cotangent, meta, w_gate, w_up, w_down)
    weights = (w_gate, w_up, w_down, *swapped)
    tok, cot, count = select(experts, top, tokz, cotz, metaz)
    tok, cot, count = slots_exchange(locals_, tok, cot, count)
    tok = tok.reshape(2, locals_ * slots, features)
    cot = cot.reshape(2, locals_ * slots, features)
    part, table = first(chips, core, tok, cot, *weights)
    shares, values = ring(chips, part.reshape(SUBS, chips, locals_ * slots // chips, part.shape[2]), table)
    out = second(core, shares.reshape(part.shape), *weights)
    back, vback = give_back(locals_, out.reshape(2, locals_, slots, 2 * features), values)
    scale = experts * nodes / (top * rows * nodes * locals_)
    summed, gates = combine(top, scale, rows, metaz, back, vback, count)
    mixed, grads, gates = finish(summed, gates)
    return mixed, grads, gates[:, :rows].T


def solution(mesh):
    chips, nodes, locals_ = mesh.shape["dp"] // 2, mesh.shape["node"], mesh.shape["local"]
    placed = (
        P(("node", "local"), "dp"),
        P(("node", "local"), "dp"),
        P(("node", "local"), None),
        P(("node", "local"), None),
        P(("node", "local"), "dp", None),
        P(("node", "local"), "dp", None),
        P(("node", "local"), None, "dp"),
    )
    return jax.shard_map(
        functools.partial(body, chips, nodes, locals_),
        mesh=mesh,
        in_specs=placed,
        out_specs=(
            P(("node", "local"), "dp"),
            P(("node", "local"), "dp"),
            P(("node", "local"), None),
        ),
        check_vma=False,
    )
```

```python
import functools

import jax
import jax.numpy as jnp
from jax import lax
from jax.experimental import pallas as pl
from jax.experimental.pallas import tpu as pltpu
from jax.sharding import PartitionSpec as P

BALANCE = 2.0
CAP = 6
USUAL = 32
SUBS = 4
STEPS = 32766.0
MESH = pl.DeviceIdType.MESH
F32, BF16 = jnp.float32, jnp.bfloat16
VMEM = pl.BlockSpec(memory_space=pltpu.VMEM)
ANY = pl.BlockSpec(memory_space=pl.ANY)
LIMIT = 56 * 1024 * 1024


def greet(peers):
    barrier = pltpu.get_barrier_semaphore()
    for peer in peers:
        pl.semaphore_signal(barrier, inc=1, device_id=peer, device_id_type=MESH)
    pl.semaphore_wait(barrier, len(peers))


def push(src, dst, send, recv, peer):
    copy = pltpu.make_async_remote_copy(
        src_ref=src, dst_ref=dst, send_sem=send, recv_sem=recv, device_id=peer, device_id_type=MESH
    )
    copy.start()
    return copy


def other_core():
    core = lax.rem(lax.axis_index("dp"), 2)
    return core, lax.axis_index("dp") + 1 - 2 * core


def upright(line, rows):
    lanes = lax.broadcasted_iota(jnp.int32, (rows, line.shape[-1]), 1)
    diagonal = lax.broadcasted_iota(jnp.int32, (rows, line.shape[-1]), 0) == lanes
    return jnp.sum(jnp.where(diagonal, line, 0.0), axis=1, keepdims=True)


def lying(column, lanes):
    rows = column.shape[0]
    lane = lax.broadcasted_iota(jnp.int32, (rows, lanes), 1)
    diagonal = lax.broadcasted_iota(jnp.int32, (rows, lanes), 0) == lane
    return jnp.sum(jnp.where(diagonal, column, 0.0), axis=0, keepdims=True)


def ring_of(axis, size):
    me = lax.axis_index(axis)
    return me, [lax.rem(me + step, size) for step in range(size)]


def spread_kernel(
    nodes, locals_, tok, cot, gates, routes, wg, wu, wd, tokz, cotl, metaz, metal, wg2, wu2, wd2,
    meta, send, recv, wsend, wrecv,
):
    node, nodes_at = ring_of("node", nodes)
    place, locals_at = ring_of("local", locals_)
    core, twin = other_core()
    top = gates.shape[1]
    for k in range(top):
        meta[k : k + 1, :] = lying(gates[:, k : k + 1], 128)
        meta[top + k : top + k + 1, :] = lying(routes[:, k : k + 1].astype(F32), 128)
    far = [{"node": at} for at in nodes_at]
    side = [{"local": at} for at in locals_at]
    greet(far[1:] + side[1:] + [{"dp": twin}])
    copies = []
    for step in range(1, max(nodes, locals_)):
        for path, (peers, me, arrays) in enumerate(
            ((far, node, ((meta, metaz), (tok, tokz))), (side, place, ((meta, metal), (cot, cotl))))
        ):
            if step < len(peers):
                for index, (src, dst) in enumerate(arrays):
                    at = (path, step - 1, index)
                    copies.append(push(src, dst.at[me], send.at[at], recv.at[at], peers[step]))
    for index, (src, dst) in enumerate(((wg, wg2), (wu, wu2), (wd, wd2))):
        copies.append(push(src.at[1 - core], dst, wsend.at[index], wrecv.at[index], {"dp": twin}))
    tokz[node] = tok[...]
    cotl[place] = cot[...]
    metaz[node] = meta[...]
    metal[place] = meta[...]
    for copy in copies:
        copy.wait()


def spread(nodes, locals_, tok, cot, gates, routes, wg, wu, wd):
    most = max(nodes, locals_) - 1
    meta = (2 * gates.shape[1], 128)
    return pl.pallas_call(
        functools.partial(spread_kernel, nodes, locals_),
        out_shape=[
            jax.ShapeDtypeStruct((nodes,) + tok.shape, BF16),
            jax.ShapeDtypeStruct((locals_,) + cot.shape, BF16),
            jax.ShapeDtypeStruct((nodes,) + meta, F32),
            jax.ShapeDtypeStruct((locals_,) + meta, F32),
        ]
        + [jax.ShapeDtypeStruct(a.shape[1:], a.dtype) for a in (wg, wu, wd)],
        in_specs=[VMEM] * 4 + [ANY] * 3,
        out_specs=[VMEM] * 4 + [ANY] * 3,
        scratch_shapes=[pltpu.VMEM(meta, F32)]
        + [pltpu.SemaphoreType.DMA((2, most, 2))] * 2
        + [pltpu.SemaphoreType.DMA((3,))] * 2,
        compiler_params=pltpu.CompilerParams(collective_id=0, has_side_effects=True, vmem_limit_bytes=LIMIT),
    )(tok, cot, gates, routes, wg, wu, wd)


def names_of(path, nodes, locals_):
    if path == 0:
        return lax.broadcasted_iota(jnp.int32, (2 * locals_, 1), 0) + 2 * locals_ * lax.axis_index("node")
    order = lax.broadcasted_iota(jnp.int32, (2 * nodes, 1), 0)
    return (order >> 1) * (2 * locals_) + (order & 1) + 2 * lax.axis_index("local")


def slot_codes(rows, top, routes, names):
    columns = routes.shape[1]
    experts = names.shape[0]
    name = jnp.broadcast_to(names.astype(F32), (experts, columns))
    chosen = jnp.zeros((experts, columns), F32)
    for k in range(top):
        chosen = chosen + jnp.where(routes[k : k + 1, :] == name, 1.0, 0.0)
    scale = -(-32768 // rows)
    earlier = lax.broadcasted_iota(jnp.int32, (columns, columns), 0)
    later = lax.broadcasted_iota(jnp.int32, (columns, columns), 1)
    block_row = (earlier * scale) >> 15
    block_col = (later * scale) >> 15
    before = jnp.where((block_row == block_col) & (earlier < later), 1.0, 0.0).astype(BF16)
    rank = jnp.dot(chosen.astype(BF16), before, preferred_element_type=F32)
    block = (lax.broadcasted_iota(jnp.int32, (experts, columns), 1) * scale >> 15).astype(F32)
    code = jnp.where(chosen > 0.0, block * CAP + rank, -1.0)
    return name, chosen, code


def lay_out(meta, top, rows):
    blocks = meta.shape[0]
    weights = jnp.concatenate([meta[i, :top, :rows] for i in range(blocks)], axis=1)
    routes = jnp.concatenate([meta[i, top : 2 * top, :rows] for i in range(blocks)], axis=1)
    return weights, routes


def select_kernel(top, nodes, locals_, tokz, cotl, metaz, metal, tok_out, cot_out, count_out):
    rows, features = tokz.shape[1:]
    for path, (src, meta, dst) in enumerate(((tokz, metaz, tok_out), (cotl, metal, cot_out))):
        experts, slots, _ = dst.shape
        _, routes = lay_out(meta, top, rows)
        columns = routes.shape[1]
        _, chosen, code = slot_codes(rows, top, routes, names_of(path, nodes, locals_))
        place = lax.broadcasted_iota(jnp.int32, (1, slots, 1), 1).astype(F32)
        pick = jnp.where(code[:, None, :] == place, 1.0, 0.0).astype(BF16).reshape(experts * slots, columns)
        got = jnp.dot(pick, src[...].reshape(columns, features), preferred_element_type=F32)
        dst[...] = got.astype(BF16).reshape(experts, slots, features)
        if path == 0:
            block = (lax.broadcasted_iota(jnp.int32, (columns, 128), 0) * -(-32768 // rows)) >> 15
            by_block = jnp.where(block == lax.broadcasted_iota(jnp.int32, (columns, 128), 1), 1.0, 0.0).astype(BF16)
            count_out[:experts, :] = jnp.dot(chosen.astype(BF16), by_block, preferred_element_type=F32)
            total = 2 * nodes * locals_
            name = lax.broadcasted_iota(jnp.int32, (total, columns), 0).astype(F32)
            hits = jnp.zeros((total, columns), F32)
            for k in range(top):
                hits = hits + jnp.where(routes[k : k + 1, :] == name, 1.0, 0.0)
            count_out[experts:, :] = jnp.broadcast_to(lying(jnp.sum(hits, axis=1, keepdims=True), 128), (8, 128))


def select(top, nodes, locals_, tokz, cotl, metaz, metal):
    features = tokz.shape[2]
    return pl.pallas_call(
        functools.partial(select_kernel, top, nodes, locals_),
        out_shape=[
            jax.ShapeDtypeStruct((2 * locals_, nodes * CAP, features), BF16),
            jax.ShapeDtypeStruct((2 * nodes, locals_ * CAP, features), BF16),
            jax.ShapeDtypeStruct((2 * locals_ + 8, 128), F32),
        ],
        in_specs=[VMEM] * 4,
        out_specs=[VMEM] * 3,
        compiler_params=pltpu.CompilerParams(vmem_limit_bytes=LIMIT),
    )(tokz, cotl, metaz, metal)


def paths_of(nodes, locals_):
    core, twin = other_core()
    ways = []
    for axis, size in (("local", locals_), ("node", nodes)):
        me, at = ring_of(axis, size)
        ways.append((me, at, [{axis: one} for one in at], [{axis: one, "dp": twin} for one in at]))
    peers = ways[0][2][1:] + ways[1][2][1:] + ways[0][3] + ways[1][3][1:]
    return core, ways, peers


def slots_kernel(nodes, locals_, tok, cot, count, tok_in, cot_in, counts, count_sum, send, recv, csend, crecv):
    core, ways, everyone = paths_of(nodes, locals_)
    greet(everyone)
    copies = []
    for step in range(1, locals_):
        copies.append(
            push(count, counts.at[ways[0][0]], csend.at[step - 1], crecv.at[step - 1], ways[0][2][step])
        )
    for step in list(range(1, max(nodes, locals_))) + [0]:
        for path, ((me, at, same, cross), src, dst) in enumerate(zip(ways, (tok, cot), (tok_in, cot_in))):
            for far, peers in enumerate((same, cross)):
                if step >= len(at) or (step == 0 and far == 0):
                    continue
                expert = 2 * at[step] + (core if far == 0 else 1 - core)
                sem = (path, step, far)
                copies.append(push(src.at[expert], dst.at[far, me], send.at[sem], recv.at[sem], peers[step]))
    for (me, _, _, _), src, dst in zip(ways, (tok, cot), (tok_in, cot_in)):
        dst[0, me] = src[2 * me + core]
    counts[ways[0][0]] = count[...]
    for copy in copies:
        copy.wait()
    count_sum[...] = jnp.sum(counts[...], axis=0)


def slots_exchange(nodes, locals_, tok, cot, count):
    most = max(nodes, locals_)
    return pl.pallas_call(
        functools.partial(slots_kernel, nodes, locals_),
        out_shape=[
            jax.ShapeDtypeStruct((2, locals_) + tok.shape[1:], BF16),
            jax.ShapeDtypeStruct((2, nodes) + cot.shape[1:], BF16),
            jax.ShapeDtypeStruct((locals_,) + count.shape, F32),
            jax.ShapeDtypeStruct(count.shape, F32),
        ],
        in_specs=[VMEM] * 3,
        out_specs=[VMEM] * 4,
        scratch_shapes=[pltpu.SemaphoreType.DMA((2, most, 2))] * 2 + [pltpu.SemaphoreType.DMA((locals_,))] * 2,
        compiler_params=pltpu.CompilerParams(collective_id=1, has_side_effects=True, vmem_limit_bytes=LIMIT),
    )(tok, cot, count)


NT = (((1,), (1,)), ((), ()))


def places(nodes, locals_, counts):
    slots = nodes * locals_ * CAP
    index = lax.broadcasted_iota(jnp.int32, (locals_, slots), 1).astype(F32)
    axis = lax.broadcasted_iota(jnp.int32, (locals_, slots), 0).astype(F32)
    lane = lax.broadcasted_iota(jnp.int32, (128, slots), 0).astype(F32)
    earlier = lax.broadcasted_iota(jnp.int32, (slots, slots), 0).astype(F32)
    rows, valid = [], None
    for path, inner in enumerate((nodes, locals_)):
        major = jnp.floor((index + 0.5) * (1.0 / (CAP * inner)))
        within = index - major * (CAP * inner)
        minor = jnp.floor((within + 0.5) * (1.0 / CAP))
        rank = within - minor * CAP
        of_node, of_local = (minor, major) if path == 0 else (major, minor)
        by_node = jnp.where(lane == of_node[:1, :], 1.0, 0.0).astype(BF16)
        count = jnp.dot(counts.astype(BF16), by_node, preferred_element_type=F32)
        count = jnp.sum(jnp.where(axis == of_local, count, 0.0), axis=0, keepdims=True)
        filled = rank[:1, :] < count
        if path == 0:
            valid = jnp.broadcast_to(jnp.where(filled, 1.0, 0.0), (8, slots)).astype(BF16)
        first_path = of_local[:1, :] * (CAP * nodes) + of_node[:1, :] * CAP + rank[:1, :]
        before = jnp.where(earlier < first_path, 1.0, 0.0).astype(BF16)
        row = jnp.dot(valid, before, preferred_element_type=F32)[:1, :]
        rows.append(jnp.where(filled, row, -1.0))
    return rows


def first_kernel(chips, nodes, locals_, at, counts, tok, cot, wg, wu, wd, wg2, wu2, wd2, out, table, rows_of):
    width = wg.shape[2]
    rows = out.shape[1]
    slots = tok.shape[1]

    @pl.when(pl.program_id(0) == 0)
    def _():
        table[...] = jnp.zeros_like(table)
        own = counts[:, pl.ds(at[1], 1), :].reshape(locals_, 128)
        row = lax.broadcasted_iota(jnp.int32, (rows, slots), 0).astype(F32)
        for path, (place, src) in enumerate(zip(places(nodes, locals_, own), (tok, cot))):
            pack = jnp.where(row == place, 1.0, 0.0).astype(BF16)
            for side in range(2):
                rows_of[path, side] = jnp.dot(pack, src[side], preferred_element_type=F32).astype(BF16)

    gate = jnp.dot(rows_of[0, 0], wg[0], preferred_element_type=F32)
    gate = gate + jnp.dot(rows_of[0, 1], wg2[...], preferred_element_type=F32)
    up = jnp.dot(rows_of[0, 0], wu[0], preferred_element_type=F32)
    up = up + jnp.dot(rows_of[0, 1], wu2[...], preferred_element_type=F32)
    back = lax.dot_general(rows_of[1, 0], wd[0], NT, preferred_element_type=F32)
    back = back + lax.dot_general(rows_of[1, 1], wd2[...], NT, preferred_element_type=F32)
    for index, value in enumerate((gate, up, back)):
        out[0, :, index * width : (index + 1) * width] = value
        top = jnp.max(jnp.abs(value).reshape(chips, -1, width), axis=1)
        table[index] = jnp.maximum(table[index], jnp.max(top, axis=1, keepdims=True))


def first(chips, nodes, locals_, rows, at, counts, tok, cot, wg, wu, wd, wg2, wu2, wd2):
    _, slots, features = tok.shape
    hidden = wg.shape[2]
    width = hidden // SUBS
    whole = pl.BlockSpec((2, slots, features), lambda s, at: (0, 0, 0))
    return pl.pallas_call(
        functools.partial(first_kernel, chips, nodes, locals_),
        out_shape=[
            jax.ShapeDtypeStruct((SUBS, rows, 3 * width), F32),
            jax.ShapeDtypeStruct((3, chips, 128), F32),
        ],
        grid_spec=pltpu.PrefetchScalarGridSpec(
            num_scalar_prefetch=1,
            grid=(SUBS,),
            in_specs=[
                pl.BlockSpec(counts.shape, lambda s, at: (0, 0, 0)),
                whole,
                whole,
                pl.BlockSpec((1, features, width), lambda s, at: (at[0], 0, s)),
                pl.BlockSpec((1, features, width), lambda s, at: (at[0], 0, s)),
                pl.BlockSpec((1, width, features), lambda s, at: (at[0], s, 0)),
                pl.BlockSpec((features, width), lambda s, at: (0, s)),
                pl.BlockSpec((features, width), lambda s, at: (0, s)),
                pl.BlockSpec((width, features), lambda s, at: (s, 0)),
            ],
            out_specs=[
                pl.BlockSpec((1, rows, 3 * width), lambda s, at: (s, 0, 0)),
                pl.BlockSpec((3, chips, 128), lambda s, at: (0, 0, 0)),
            ],
            scratch_shapes=[pltpu.VMEM((2, 2, rows, features), BF16)],
        ),
        compiler_params=pltpu.CompilerParams(vmem_limit_bytes=LIMIT),
    )(at, counts, tok, cot, wg, wu, wd, wg2, wu2, wd2)


def ring_kernel(
    chips, part, table, shares, values, got, stage, bounds, bounds_in, rsend, rrecv, gsend, grecv, vsend, vrecv, tsend, trecv
):
    dp = lax.axis_index("dp")
    core = lax.rem(dp, 2)
    me = (dp - core) // 2
    depth = chips // 2
    half = SUBS // 2
    width = part.shape[3] // 3
    rows = part.shape[2]

    def chip(offset):
        return lax.rem(me + offset + 2 * chips, chips)

    way = [{"dp": 2 * chip(1) + core}, {"dp": 2 * chip(-1) + core}]
    sign = (1, -1)
    greet(way)

    def halves(direction):
        return range(half) if direction == 0 else range(half, SUBS)

    copies = []

    def bound(ref, chunk):
        lines = [jnp.broadcast_to(ref[index, pl.ds(chunk, 1), :], (1, 128)) for index in range(3)]
        return jnp.concatenate([line for line in lines for _ in range(width // 128)], axis=1)

    def reduce_send(direction, step, sub, total, chunk):
        at = (direction, step, sub)
        limit = bound(bounds.at[direction, step], chunk)
        inverse = jnp.where(limit > 1e-30, STEPS / jnp.maximum(limit, 1e-30), 0.0)
        stage[at] = jnp.round(total * inverse).astype(jnp.int32).astype(jnp.int16)
        copies.append(push(stage.at[at], got.at[at], rsend.at[at], rrecv.at[at], way[direction]))

    def reduce_wait(direction, step, sub, chunk):
        at = (direction, step, sub)
        pltpu.make_async_copy(got.at[at], got.at[at], rrecv.at[at]).wait()
        limit = bound(bounds_in.at[direction, step], chunk)
        return got[at].astype(jnp.int32).astype(F32) * (limit * (1.0 / STEPS))

    def bound_send(direction, step):
        at = (direction, step)
        copies.append(push(bounds.at[at], bounds_in.at[at], tsend.at[at], trecv.at[at], way[direction]))

    def bound_wait(direction, step):
        at = (direction, step)
        pltpu.make_async_copy(bounds_in.at[at], bounds_in.at[at], trecv.at[at]).wait()

    for direction in range(2):
        bounds[direction, 0] = table[...]
        bound_send(direction, 0)
    for index in range(half):
        for direction in range(2):
            sub = halves(direction)[index]
            chunk = chip(sign[direction] * depth)
            reduce_send(direction, 0, sub, part[sub, chunk], chunk)
    for step in range(1, depth):
        for direction in range(2):
            bound_wait(direction, step - 1)
            bounds[direction, step] = table[...] + bounds_in[direction, step - 1]
            bound_send(direction, step)
        for index in range(half):
            for direction in range(2):
                if step == 1:
                    sub = halves(1 - direction)[index]
                    chunk = chip(sign[direction] * (depth - 1))
                    reduce_send(direction, 1, sub, part[sub, chunk], chunk)
        for sub in range(SUBS):
            for direction in range(2):
                if step == 1 and sub not in halves(direction):
                    continue
                chunk = chip(sign[direction] * (depth - step))
                total = part[sub, chunk] + reduce_wait(direction, step - 1, sub, chunk)
                reduce_send(direction, step, sub, total, chunk)
    for direction in range(2):
        bound_wait(direction, depth - 1)

    def gather_send(direction, step, sub):
        chunk = shares.at[sub, chip(-sign[direction] * step)]
        at = (direction, step, sub)
        copies.append(push(chunk, chunk, gsend.at[at], grecv.at[at], way[direction]))

    def gather_wait(direction, step, sub):
        chunk = shares.at[sub, chip(-sign[direction] * (step + 1))]
        pltpu.make_async_copy(chunk, chunk, grecv.at[direction, step, sub]).wait()

    def value_send(direction, step):
        chunk = values.at[chip(-sign[direction] * step)]
        at = (direction, step)
        copies.append(push(chunk, chunk, vsend.at[at], vrecv.at[at], way[direction]))

    def value_wait(direction, step):
        chunk = values.at[chip(-sign[direction] * (step + 1))]
        pltpu.make_async_copy(chunk, chunk, vrecv.at[direction, step]).wait()

    inner = jnp.zeros((rows, 1), F32)
    for index in range(half):
        for sub in (halves(0)[index], halves(1)[index]):
            total = part[sub, me]
            for direction in range(2):
                if depth > 1 or sub in halves(direction):
                    total = total + reduce_wait(direction, depth - 1, sub, me)
            gate, up, back = total[:, :width], total[:, width : 2 * width], total[:, 2 * width :]
            logistic = 1.0 / (1.0 + jnp.exp(-gate))
            active = gate * logistic
            hidden = (active * up).astype(BF16)
            shares[sub, me, :, :width] = hidden
            d_gate = back * up * logistic * (1.0 + gate * (1.0 - logistic))
            shares[sub, me, :, width : 2 * width] = d_gate.astype(BF16)
            shares[sub, me, :, 2 * width :] = (back * active).astype(BF16)
            for direction in range(2):
                if depth > 1 or sub in halves(direction):
                    gather_send(direction, 0, sub)
            inner = inner + jnp.sum(hidden.astype(F32) * back, axis=1, keepdims=True)
    lanes = lax.broadcasted_iota(jnp.int32, (rows, 128), 1)
    diagonal = lax.broadcasted_iota(jnp.int32, (rows, 128), 0) == lanes
    line = jnp.sum(jnp.where(diagonal, inner, 0.0), axis=0, keepdims=True)
    values[me] = jnp.broadcast_to(line, (8, 128))
    for direction in range(2):
        if depth > 1 or direction == 0:
            value_send(direction, 0)
    for step in range(1, depth + 1):
        last = step == depth
        for index in range(half):
            for sub in (halves(0)[index], halves(1)[index]):
                for direction in range(2):
                    if last and sub not in halves(direction):
                        continue
                    gather_wait(direction, step - 1, sub)
                    if not last and (step < depth - 1 or sub in halves(direction)):
                        gather_send(direction, step, sub)
        for direction in range(2):
            if last and direction == 1:
                continue
            value_wait(direction, step - 1)
            if not last and (step < depth - 1 or direction == 0):
                value_send(direction, step)
    for copy in copies:
        copy.wait_send()


def ring(chips, ident, part, table):
    _, _, rows, wide = part.shape
    depth = chips // 2
    return pl.pallas_call(
        functools.partial(ring_kernel, chips),
        out_shape=[jax.ShapeDtypeStruct(part.shape, BF16), jax.ShapeDtypeStruct((chips, 8, 128), F32)],
        in_specs=[VMEM] * 2,
        out_specs=[VMEM] * 2,
        scratch_shapes=[pltpu.VMEM((2, depth, SUBS, rows, wide), jnp.int16)] * 2
        + [pltpu.VMEM((2, depth) + table.shape, F32)] * 2
        + [pltpu.SemaphoreType.DMA((2, depth, SUBS))] * 4
        + [pltpu.SemaphoreType.DMA((2, depth))] * 4,
        compiler_params=pltpu.CompilerParams(collective_id=ident, has_side_effects=True, vmem_limit_bytes=LIMIT),
    )(part, table)


def second_kernel(nodes, locals_, at, counts, shares, values, wg, wu, wd, wg2, wu2, wd2, forward_out, back_out, values_out):
    features = wg2.shape[0]
    width = wg2.shape[1] // SUBS
    rows = shares.shape[1]
    slots = forward_out.shape[1]
    own = counts[:, pl.ds(at[1], 1), :].reshape(locals_, 128)
    place = places(nodes, locals_, own)
    row = lax.broadcasted_iota(jnp.int32, (slots, rows), 1).astype(F32)
    unpack = [jnp.where(row == upright(one, slots), 1.0, 0.0).astype(BF16) for one in place]
    for side, (gate, up, down) in enumerate(((wg.at[0], wu.at[0], wd.at[0]), (wg2, wu2, wd2))):
        forward = jnp.zeros((rows, features), F32)
        back = forward
        for sub in range(SUBS):
            units = slice(sub * width, (sub + 1) * width)
            forward = forward + jnp.dot(shares[sub, :, :width], down[units, :], preferred_element_type=F32)
            back = back + lax.dot_general(
                shares[sub, :, width : 2 * width], gate[:, units], NT, preferred_element_type=F32
            )
            back = back + lax.dot_general(shares[sub, :, 2 * width :], up[:, units], NT, preferred_element_type=F32)
        for matrix, value, out in ((unpack[0], forward, forward_out), (unpack[1], back, back_out)):
            out[side] = jnp.dot(matrix, value.astype(BF16), preferred_element_type=F32).astype(BF16)
    chips = values.shape[0]
    share = rows // chips
    value = jnp.concatenate([upright(values[chip, 0:1, :], share) for chip in range(chips)], axis=0)
    row = lax.broadcasted_iota(jnp.int32, (rows, slots), 0).astype(F32)
    value = jnp.sum(jnp.where(row == place[0], value, 0.0), axis=0, keepdims=True)
    values_out[...] = jnp.zeros_like(values_out)
    part = slots // locals_
    for relay in range(locals_):
        values_out[relay, :, :part] = jnp.broadcast_to(value[:, relay * part : (relay + 1) * part], (8, part))


def second(nodes, locals_, at, counts, shares, values, wg, wu, wd, wg2, wu2, wd2):
    _, rows, wide = shares.shape
    features, hidden = wg2.shape
    slots = nodes * locals_ * CAP
    side = pl.BlockSpec((features, hidden), lambda i, at: (0, 0))
    out = jax.ShapeDtypeStruct((2, slots, features), BF16)
    return pl.pallas_call(
        functools.partial(second_kernel, nodes, locals_),
        out_shape=[out, out, jax.ShapeDtypeStruct((locals_, 8, 128), F32)],
        grid_spec=pltpu.PrefetchScalarGridSpec(
            num_scalar_prefetch=1,
            grid=(1,),
            in_specs=[
                pl.BlockSpec(counts.shape, lambda i, at: (0, 0, 0)),
                pl.BlockSpec((SUBS, rows, wide), lambda i, at: (0, 0, 0)),
                pl.BlockSpec(values.shape, lambda i, at: (0, 0, 0)),
                pl.BlockSpec((1, features, hidden), lambda i, at: (at[0], 0, 0)),
                pl.BlockSpec((1, features, hidden), lambda i, at: (at[0], 0, 0)),
                pl.BlockSpec((1, hidden, features), lambda i, at: (at[0], 0, 0)),
                side,
                side,
                pl.BlockSpec((hidden, features), lambda i, at: (0, 0)),
            ],
            out_specs=[
                pl.BlockSpec((2, slots, features), lambda i, at: (0, 0, 0)),
                pl.BlockSpec((2, slots, features), lambda i, at: (0, 0, 0)),
                pl.BlockSpec((locals_, 8, 128), lambda i, at: (0, 0, 0)),
            ],
        ),
        compiler_params=pltpu.CompilerParams(vmem_limit_bytes=LIMIT),
    )(at, counts, shares, values, wg, wu, wd, wg2, wu2, wd2)


def return_kernel(nodes, locals_, forward, back, values, forward_in, back_in, values_in, send, recv, vsend, vrecv):
    core, ways, everyone = paths_of(nodes, locals_)
    greet(everyone)
    copies = []
    for step in list(range(1, max(nodes, locals_))) + [0]:
        for path, ((me, at, same, cross), src, dst) in enumerate(zip(ways, (forward, back), (forward_in, back_in))):
            mine = 2 * me + core
            for far, peers in enumerate((same, cross)):
                if step >= len(at) or (step == 0 and far == 0):
                    continue
                sem = (path, step, far)
                copies.append(push(src.at[far, at[step]], dst.at[mine], send.at[sem], recv.at[sem], peers[step]))
                if path == 0:
                    sem = (step, far)
                    line = values.at[at[step]]
                    copies.append(push(line, values_in.at[mine], vsend.at[sem], vrecv.at[sem], peers[step]))
    for (me, _, _, _), src, dst in zip(ways, (forward, back), (forward_in, back_in)):
        dst[2 * me + core] = src[0, me]
    me = ways[0][0]
    values_in[2 * me + core] = values[me]
    for copy in copies:
        copy.wait()


def give_back(nodes, locals_, forward, back, values):
    most = max(nodes, locals_)
    return pl.pallas_call(
        functools.partial(return_kernel, nodes, locals_),
        out_shape=[
            jax.ShapeDtypeStruct((2 * locals_,) + forward.shape[2:], BF16),
            jax.ShapeDtypeStruct((2 * nodes,) + back.shape[2:], BF16),
            jax.ShapeDtypeStruct((2 * locals_, 8, 128), F32),
        ],
        in_specs=[VMEM] * 3,
        out_specs=[VMEM] * 3,
        scratch_shapes=[pltpu.SemaphoreType.DMA((2, most, 2))] * 2 + [pltpu.SemaphoreType.DMA((locals_, 2))] * 2,
        compiler_params=pltpu.CompilerParams(collective_id=3, has_side_effects=True, vmem_limit_bytes=LIMIT),
    )(forward, back, values)


def combine_kernel(top, nodes, locals_, scale, metaz, metal, forward, back, vback, count, forward_out, back_out, gates_out):
    rows = forward_out.shape[1]
    for path, (meta, src, out) in enumerate(((metaz, forward, forward_out), (metal, back, back_out))):
        experts, slots, wide = src.shape
        weights, routes = lay_out(meta, top, rows)
        columns = routes.shape[1]
        name, _, code = slot_codes(rows, top, routes, names_of(path, nodes, locals_))
        weight = jnp.zeros((experts, columns), F32)
        for k in range(top):
            weight = weight + jnp.where(routes[k : k + 1, :] == name, weights[k : k + 1, :], 0.0)
        place = lax.broadcasted_iota(jnp.int32, (1, slots, 1), 1).astype(F32)
        hit = code[:, None, :] == place
        rows_back = src[...].reshape(experts * slots, wide)
        high = weight.astype(BF16).astype(F32)
        total = jnp.zeros((columns, wide), F32)
        for share in (high, weight - high):
            spread_ = jnp.where(hit, share[:, None, :], 0.0).astype(BF16).reshape(experts * slots, columns)
            total = total + lax.dot_general(spread_, rows_back, (((0,), (0,)), ((), ())), preferred_element_type=F32)
        out[...] = total.astype(BF16).reshape(out.shape)
        if path == 0:
            lanes = lax.broadcasted_iota(jnp.int32, (experts, slots, 128), 2)
            diagonal = lax.broadcasted_iota(jnp.int32, (experts, slots, 128), 1) == lanes
            value = jnp.sum(jnp.where(diagonal, vback[:, 0:1, :], 0.0), axis=2, keepdims=True)
            inner = jnp.sum(jnp.where(hit, value, 0.0), axis=1)
            number = jnp.sum(count[:experts, :], axis=1, keepdims=True)
            inner = inner + BALANCE * scale * number
            gates = [
                jnp.sum(jnp.where(routes[k : k + 1, :] == name, inner, 0.0), axis=0, keepdims=True)
                for k in range(top)
            ]
            gates = jnp.concatenate(gates, axis=0)
            gates_out[...] = jnp.zeros_like(gates_out)
            for i in range(nodes):
                gates_out[i, :, :rows] = gates[:, i * rows : (i + 1) * rows]


def combine(top, nodes, locals_, scale, rows, metaz, metal, forward, back, vback, count):
    return pl.pallas_call(
        functools.partial(combine_kernel, top, nodes, locals_, scale),
        out_shape=[
            jax.ShapeDtypeStruct((nodes, rows, forward.shape[2]), BF16),
            jax.ShapeDtypeStruct((locals_, rows, back.shape[2]), BF16),
            jax.ShapeDtypeStruct((nodes, top, 128), F32),
        ],
        in_specs=[VMEM] * 6,
        out_specs=[VMEM] * 3,
        compiler_params=pltpu.CompilerParams(vmem_limit_bytes=LIMIT),
    )(metaz, metal, forward, back, vback, count)


def home_kernel(nodes, locals_, forward, back, gates, forward_in, back_in, gates_in, send, recv):
    node, nodes_at = ring_of("node", nodes)
    place, locals_at = ring_of("local", locals_)
    far = [{"node": at} for at in nodes_at]
    side = [{"local": at} for at in locals_at]
    greet(far[1:] + side[1:])
    copies = []
    for step in range(1, max(nodes, locals_)):
        for index, (src, dst, at, peers) in enumerate(
            (
                (gates, gates_in, nodes_at, far),
                (forward, forward_in, nodes_at, far),
                (back, back_in, locals_at, side),
            )
        ):
            if step < len(peers):
                sem = (step - 1, index)
                copies.append(push(src.at[at[step]], dst.at[step], send.at[sem], recv.at[sem], peers[step]))
    for src, dst, me in ((gates, gates_in, node), (forward, forward_in, node), (back, back_in, place)):
        dst[0] = src[me]
    for copy in copies:
        copy.wait()


def home(nodes, locals_, forward, back, gates):
    most = max(nodes, locals_) - 1
    return pl.pallas_call(
        functools.partial(home_kernel, nodes, locals_),
        out_shape=[jax.ShapeDtypeStruct(a.shape, a.dtype) for a in (forward, back, gates)],
        in_specs=[VMEM] * 3,
        out_specs=[VMEM] * 3,
        scratch_shapes=[pltpu.SemaphoreType.DMA((most, 3))] * 2,
        compiler_params=pltpu.CompilerParams(collective_id=4, has_side_effects=True, vmem_limit_bytes=LIMIT),
    )(forward, back, gates)


def total_kernel(forward, back, gates, mixed, grads, gates_out):
    mixed[...] = jnp.sum(forward[...].astype(F32), axis=0).astype(BF16)
    grads[...] = jnp.sum(back[...].astype(F32), axis=0).astype(BF16)
    gate = jnp.sum(gates[...], axis=0)
    for k in range(gates_out.shape[1]):
        gates_out[:, k : k + 1] = upright(gate[k : k + 1, :], gates_out.shape[0])


def total(forward, back, gates):
    _, rows, features = forward.shape
    half = jax.ShapeDtypeStruct((rows, features), BF16)
    return pl.pallas_call(
        total_kernel,
        out_shape=[half, half, jax.ShapeDtypeStruct((rows, gates.shape[1]), F32)],
        in_specs=[VMEM] * 3,
        out_specs=[VMEM] * 3,
        compiler_params=pltpu.CompilerParams(vmem_limit_bytes=LIMIT),
    )(forward, back, gates)


def middle(chips, nodes, locals_, rows, ident, at, counts, tok, cot, *weights):
    part, table = first(chips, nodes, locals_, rows, at, counts, tok, cot, *weights)
    shares, values = ring(chips, ident, part.reshape(SUBS, chips, rows // chips, part.shape[2]), table)
    return second(nodes, locals_, at, counts, shares.reshape(part.shape), values, *weights)


def body(chips, nodes, locals_, tokens, cotangent, routes, gate_weights, w_gate, w_up, w_down):
    rows, features = tokens.shape
    top = routes.shape[1]
    slots = nodes * locals_ * CAP
    core = lax.rem(lax.axis_index("dp"), 2)
    at = jnp.stack([core, 2 * lax.axis_index("local") + core]).astype(jnp.int32)
    tokz, cotl, metaz, metal, *swapped = spread(
        nodes, locals_, tokens, cotangent, gate_weights, routes, w_gate, w_up, w_down
    )
    tok, cot, count = select(top, nodes, locals_, tokz, cotl, metaz, metal)
    tok, cot, counts, count_sum = slots_exchange(nodes, locals_, tok, cot, count)
    inputs = (
        at, counts, tok.reshape(2, slots, features), cot.reshape(2, slots, features), w_gate, w_up, w_down, *swapped
    )
    usual = functools.partial(middle, chips, nodes, locals_, USUAL * chips, 2)
    every = functools.partial(middle, chips, nodes, locals_, slots, 5)
    crowded = jnp.max(count_sum[2 * locals_ :, :]) > USUAL * chips
    forward, back, values = lax.cond(crowded, every, usual, *inputs)
    forward = forward.reshape(2, locals_, nodes * CAP, features)
    back = back.reshape(2, nodes, locals_ * CAP, features)
    forward, back, values = give_back(nodes, locals_, forward, back, values)
    scale = 2 * nodes * locals_ / (top * rows * nodes * locals_)
    summed = combine(top, nodes, locals_, scale, rows, metaz, metal, forward, back, values, count_sum)
    return total(*home(nodes, locals_, *summed))


def solution(mesh):
    chips, nodes, locals_ = mesh.shape["dp"] // 2, mesh.shape["node"], mesh.shape["local"]
    placed = (
        P(("node", "local"), "dp"),
        P(("node", "local"), "dp"),
        P(("node", "local"), None),
        P(("node", "local"), None),
        P(("node", "local"), "dp", None),
        P(("node", "local"), "dp", None),
        P(("node", "local"), None, "dp"),
    )
    return jax.shard_map(
        functools.partial(body, chips, nodes, locals_),
        mesh=mesh,
        in_specs=placed,
        out_specs=(
            P(("node", "local"), "dp"),
            P(("node", "local"), "dp"),
            P(("node", "local"), None),
        ),
        check_vma=False,
    )
```

```python
import functools

import jax
import jax.numpy as jnp
from jax import lax
from jax.experimental import pallas as pl
from jax.experimental.pallas import tpu as pltpu
from jax.sharding import PartitionSpec as P

BALANCE = 2.0
CAP = 6
USUAL = 32
SUBS = 4
STEPS = 32766.0
MESH = pl.DeviceIdType.MESH
F32, BF16 = jnp.float32, jnp.bfloat16
VMEM = pl.BlockSpec(memory_space=pltpu.VMEM)
ANY = pl.BlockSpec(memory_space=pl.ANY)
LIMIT = 56 * 1024 * 1024


def greet(peers):
    barrier = pltpu.get_barrier_semaphore()
    for peer in peers:
        pl.semaphore_signal(barrier, inc=1, device_id=peer, device_id_type=MESH)
    pl.semaphore_wait(barrier, len(peers))


def push(src, dst, send, recv, peer):
    copy = pltpu.make_async_remote_copy(
        src_ref=src, dst_ref=dst, send_sem=send, recv_sem=recv, device_id=peer, device_id_type=MESH
    )
    copy.start()
    return copy


def other_core():
    core = lax.rem(lax.axis_index("dp"), 2)
    return core, lax.axis_index("dp") + 1 - 2 * core


def upright(line, rows):
    lanes = lax.broadcasted_iota(jnp.int32, (rows, line.shape[-1]), 1)
    diagonal = lax.broadcasted_iota(jnp.int32, (rows, line.shape[-1]), 0) == lanes
    return jnp.sum(jnp.where(diagonal, line, 0.0), axis=1, keepdims=True)


def lying(column, lanes):
    rows = column.shape[0]
    lane = lax.broadcasted_iota(jnp.int32, (rows, lanes), 1)
    diagonal = lax.broadcasted_iota(jnp.int32, (rows, lanes), 0) == lane
    return jnp.sum(jnp.where(diagonal, column, 0.0), axis=0, keepdims=True)


def ring_of(axis, size):
    me = lax.axis_index(axis)
    return me, [lax.rem(me + step, size) for step in range(size)]


def names_of(path, nodes, locals_):
    if path == 0:
        return lax.broadcasted_iota(jnp.int32, (2 * locals_, 1), 0) + 2 * locals_ * lax.axis_index("node")
    order = lax.broadcasted_iota(jnp.int32, (2 * nodes, 1), 0)
    return (order >> 1) * (2 * locals_) + (order & 1) + 2 * lax.axis_index("local")


def slot_codes(rows, top, routes, names):
    columns = routes.shape[1]
    experts = names.shape[0]
    name = jnp.broadcast_to(names.astype(F32), (experts, columns))
    chosen = jnp.zeros((experts, columns), F32)
    for k in range(top):
        chosen = chosen + jnp.where(routes[k : k + 1, :] == name, 1.0, 0.0)
    scale = -(-32768 // rows)
    earlier = lax.broadcasted_iota(jnp.int32, (columns, columns), 0)
    later = lax.broadcasted_iota(jnp.int32, (columns, columns), 1)
    block_row = (earlier * scale) >> 15
    block_col = (later * scale) >> 15
    before = jnp.where((block_row == block_col) & (earlier < later), 1.0, 0.0).astype(BF16)
    rank = jnp.dot(chosen.astype(BF16), before, preferred_element_type=F32)
    block = (lax.broadcasted_iota(jnp.int32, (experts, columns), 1) * scale >> 15).astype(F32)
    code = jnp.where(chosen > 0.0, block * CAP + rank, -1.0)
    return name, chosen, code


def lay_out(meta, top, rows):
    blocks = meta.shape[0]
    weights = jnp.concatenate([meta[i, :top, :rows] for i in range(blocks)], axis=1)
    routes = jnp.concatenate([meta[i, top : 2 * top, :rows] for i in range(blocks)], axis=1)
    return weights, routes


def paths_of(nodes, locals_):
    core, twin = other_core()
    ways = []
    for axis, size in (("local", locals_), ("node", nodes)):
        me, at = ring_of(axis, size)
        ways.append((me, at, [{axis: one} for one in at], [{axis: one, "dp": twin} for one in at]))
    peers = ways[0][2][1:] + ways[1][2][1:] + ways[0][3] + ways[1][3][1:]
    return core, ways, peers


def choose(path, top, nodes, locals_, src, meta, dst, count):
    rows, features = src.shape[1:]
    experts, slots, _ = dst.shape
    _, routes = lay_out(meta, top, rows)
    columns = routes.shape[1]
    _, chosen, code = slot_codes(rows, top, routes, names_of(path, nodes, locals_))
    place = lax.broadcasted_iota(jnp.int32, (1, slots, 1), 1).astype(F32)
    pick = jnp.where(code[:, None, :] == place, 1.0, 0.0).astype(BF16).reshape(experts * slots, columns)
    got = jnp.dot(pick, src[...].reshape(columns, features), preferred_element_type=F32)
    dst[...] = got.astype(BF16).reshape(experts, slots, features)
    if path == 0:
        block = (lax.broadcasted_iota(jnp.int32, (columns, 128), 0) * -(-32768 // rows)) >> 15
        by_block = jnp.where(block == lax.broadcasted_iota(jnp.int32, (columns, 128), 1), 1.0, 0.0).astype(BF16)
        count[:experts, :] = jnp.dot(chosen.astype(BF16), by_block, preferred_element_type=F32)
        total = 2 * nodes * locals_
        name = lax.broadcasted_iota(jnp.int32, (total, columns), 0).astype(F32)
        hits = jnp.zeros((total, columns), F32)
        for k in range(top):
            hits = hits + jnp.where(routes[k : k + 1, :] == name, 1.0, 0.0)
        count[experts:, :] = jnp.broadcast_to(lying(jnp.sum(hits, axis=1, keepdims=True), 128), (8, 128))


def front_kernel(
    nodes, locals_, tok, cot, gates, routes, wg, wu, wd,
    tok_in, cot_in, counts, count_sum, metaz, metal, wg2, wu2, wd2,
    meta, tokz, cotl, tok_out, cot_out, count, send, recv, wsend, wrecv, ssend, srecv, csend, crecv,
):
    node, nodes_at = ring_of("node", nodes)
    place, locals_at = ring_of("local", locals_)
    core, twin = other_core()
    top, rows = gates.shape
    meta[...] = jnp.zeros_like(meta)
    meta[:top, :rows] = gates[...]
    meta[top:, :rows] = routes[...].astype(F32)
    far = [{"node": at} for at in nodes_at]
    side = [{"local": at} for at in locals_at]
    core, ways, everyone = paths_of(nodes, locals_)
    greet(everyone)
    blocks = [[], []]
    for step in range(1, max(nodes, locals_)):
        for path, (peers, me, arrays) in enumerate(
            ((far, node, ((meta, metaz), (tok, tokz))), (side, place, ((meta, metal), (cot, cotl))))
        ):
            if step < len(peers):
                for index, (src, dst) in enumerate(arrays):
                    at = (path, step - 1, index)
                    blocks[path].append(push(src, dst.at[me], send.at[at], recv.at[at], peers[step]))
    tokz[node] = tok[...]
    cotl[place] = cot[...]
    metaz[node] = meta[...]
    metal[place] = meta[...]
    copies = []
    for path, (src, met, out, dst) in enumerate(((tokz, metaz, tok_out, tok_in), (cotl, metal, cot_out, cot_in))):
        for copy in blocks[path]:
            copy.wait_recv()
        choose(path, top, nodes, locals_, src, met, out, count)
        me, at, same, cross = ways[path]
        if path == 0:
            for step in range(1, locals_):
                sem = step - 1
                copies.append(push(count, counts.at[me], csend.at[sem], crecv.at[sem], same[step]))
        for step in list(range(1, len(at))) + [0]:
            for distant, peers in enumerate((same, cross)):
                if step == 0 and distant == 0:
                    continue
                expert = 2 * at[step] + (core if distant == 0 else 1 - core)
                sem = (path, step, distant)
                copies.append(push(out.at[expert], dst.at[distant, me], ssend.at[sem], srecv.at[sem], peers[step]))
        dst[0, me] = out[2 * me + core]
    counts[place] = count[...]
    for index, (src, dst) in enumerate(((wg, wg2), (wu, wu2), (wd, wd2))):
        copies.append(push(src.at[1 - core], dst, wsend.at[index], wrecv.at[index], {"dp": twin}))
    for copy in copies:
        copy.wait()
    for path in range(2):
        for copy in blocks[path]:
            copy.wait_send()
    count_sum[...] = jnp.sum(counts[...], axis=0)


def front(nodes, locals_, tok, cot, gates, routes, wg, wu, wd):
    features = tok.shape[1]
    most = max(nodes, locals_)
    meta = (2 * gates.shape[0], 128)
    count = (2 * locals_ + 8, 128)
    return pl.pallas_call(
        functools.partial(front_kernel, nodes, locals_),
        out_shape=[
            jax.ShapeDtypeStruct((2, locals_, nodes * CAP, features), BF16),
            jax.ShapeDtypeStruct((2, nodes, locals_ * CAP, features), BF16),
            jax.ShapeDtypeStruct((locals_,) + count, F32),
            jax.ShapeDtypeStruct(count, F32),
            jax.ShapeDtypeStruct((nodes,) + meta, F32),
            jax.ShapeDtypeStruct((locals_,) + meta, F32),
        ]
        + [jax.ShapeDtypeStruct(a.shape[1:], a.dtype) for a in (wg, wu, wd)],
        in_specs=[VMEM] * 4 + [ANY] * 3,
        out_specs=[VMEM] * 6 + [ANY] * 3,
        scratch_shapes=[
            pltpu.VMEM(meta, F32),
            pltpu.VMEM((nodes,) + tok.shape, BF16),
            pltpu.VMEM((locals_,) + cot.shape, BF16),
            pltpu.VMEM((2 * locals_, nodes * CAP, features), BF16),
            pltpu.VMEM((2 * nodes, locals_ * CAP, features), BF16),
            pltpu.VMEM(count, F32),
        ]
        + [pltpu.SemaphoreType.DMA((2, most, 2))] * 2
        + [pltpu.SemaphoreType.DMA((3,))] * 2
        + [pltpu.SemaphoreType.DMA((2, most, 2))] * 2
        + [pltpu.SemaphoreType.DMA((locals_,))] * 2,
        compiler_params=pltpu.CompilerParams(collective_id=0, has_side_effects=True, vmem_limit_bytes=LIMIT),
    )(tok, cot, gates, routes, wg, wu, wd)


NT = (((1,), (1,)), ((), ()))


def places(nodes, locals_, counts):
    slots = nodes * locals_ * CAP
    index = lax.broadcasted_iota(jnp.int32, (locals_, slots), 1).astype(F32)
    axis = lax.broadcasted_iota(jnp.int32, (locals_, slots), 0).astype(F32)
    lane = lax.broadcasted_iota(jnp.int32, (128, slots), 0).astype(F32)
    earlier = lax.broadcasted_iota(jnp.int32, (slots, slots), 0).astype(F32)
    rows, valid = [], None
    for path, inner in enumerate((nodes, locals_)):
        major = jnp.floor((index + 0.5) * (1.0 / (CAP * inner)))
        within = index - major * (CAP * inner)
        minor = jnp.floor((within + 0.5) * (1.0 / CAP))
        rank = within - minor * CAP
        of_node, of_local = (minor, major) if path == 0 else (major, minor)
        by_node = jnp.where(lane == of_node[:1, :], 1.0, 0.0).astype(BF16)
        count = jnp.dot(counts.astype(BF16), by_node, preferred_element_type=F32)
        count = jnp.sum(jnp.where(axis == of_local, count, 0.0), axis=0, keepdims=True)
        filled = rank[:1, :] < count
        if path == 0:
            valid = jnp.broadcast_to(jnp.where(filled, 1.0, 0.0), (8, slots)).astype(BF16)
        first_path = of_local[:1, :] * (CAP * nodes) + of_node[:1, :] * CAP + rank[:1, :]
        before = jnp.where(earlier < first_path, 1.0, 0.0).astype(BF16)
        row = jnp.dot(valid, before, preferred_element_type=F32)[:1, :]
        rows.append(jnp.where(filled, row, -1.0))
    return rows


def ring_way(chips):
    core, _ = other_core()
    me = (lax.axis_index("dp") - core) // 2
    return me, [{"dp": 2 * lax.rem(me + step + chips, chips) + core} for step in (1, -1)]


def ring_steps(
    chips, part, table, shares, values, got, stage, bounds, bounds_in, rsend, rrecv, gsend, grecv, vsend, vrecv, tsend, trecv
):
    me, way = ring_way(chips)
    depth = chips // 2
    half = SUBS // 2
    width = part.shape[3] // 3
    rows = part.shape[2]

    def chip(offset):
        return lax.rem(me + offset + 2 * chips, chips)

    sign = (1, -1)

    def halves(direction):
        return range(half) if direction == 0 else range(half, SUBS)

    copies = []

    def bound(ref, chunk):
        lines = [jnp.broadcast_to(ref[index, pl.ds(chunk, 1), :], (1, 128)) for index in range(3)]
        return jnp.concatenate([line for line in lines for _ in range(width // 128)], axis=1)

    def reduce_send(direction, step, sub, total, chunk):
        at = (direction, step, sub)
        limit = bound(bounds.at[direction, step], chunk)
        inverse = jnp.where(limit > 1e-30, STEPS / jnp.maximum(limit, 1e-30), 0.0)
        stage[at] = jnp.round(total * inverse).astype(jnp.int32).astype(jnp.int16)
        copies.append(push(stage.at[at], got.at[at], rsend.at[at], rrecv.at[at], way[direction]))

    def reduce_wait(direction, step, sub, chunk):
        at = (direction, step, sub)
        pltpu.make_async_copy(got.at[at], got.at[at], rrecv.at[at]).wait()
        limit = bound(bounds_in.at[direction, step], chunk)
        return got[at].astype(jnp.int32).astype(F32) * (limit * (1.0 / STEPS))

    def bound_send(direction, step):
        at = (direction, step)
        copies.append(push(bounds.at[at], bounds_in.at[at], tsend.at[at], trecv.at[at], way[direction]))

    def bound_wait(direction, step):
        at = (direction, step)
        pltpu.make_async_copy(bounds_in.at[at], bounds_in.at[at], trecv.at[at]).wait()

    for direction in range(2):
        bounds[direction, 0] = table[...]
        bound_send(direction, 0)
    for index in range(half):
        for direction in range(2):
            sub = halves(direction)[index]
            chunk = chip(sign[direction] * depth)
            reduce_send(direction, 0, sub, part[sub, chunk], chunk)
    for step in range(1, depth):
        for direction in range(2):
            bound_wait(direction, step - 1)
            bounds[direction, step] = table[...] + bounds_in[direction, step - 1]
            bound_send(direction, step)
        for index in range(half):
            for direction in range(2):
                if step == 1:
                    sub = halves(1 - direction)[index]
                    chunk = chip(sign[direction] * (depth - 1))
                    reduce_send(direction, 1, sub, part[sub, chunk], chunk)
        for sub in range(SUBS):
            for direction in range(2):
                if step == 1 and sub not in halves(direction):
                    continue
                chunk = chip(sign[direction] * (depth - step))
                total = part[sub, chunk] + reduce_wait(direction, step - 1, sub, chunk)
                reduce_send(direction, step, sub, total, chunk)
    for direction in range(2):
        bound_wait(direction, depth - 1)

    def gather_send(direction, step, sub):
        chunk = shares.at[sub, chip(-sign[direction] * step)]
        at = (direction, step, sub)
        copies.append(push(chunk, chunk, gsend.at[at], grecv.at[at], way[direction]))

    def gather_wait(direction, step, sub):
        chunk = shares.at[sub, chip(-sign[direction] * (step + 1))]
        pltpu.make_async_copy(chunk, chunk, grecv.at[direction, step, sub]).wait()

    def value_send(direction, step):
        chunk = values.at[chip(-sign[direction] * step)]
        at = (direction, step)
        copies.append(push(chunk, chunk, vsend.at[at], vrecv.at[at], way[direction]))

    def value_wait(direction, step):
        chunk = values.at[chip(-sign[direction] * (step + 1))]
        pltpu.make_async_copy(chunk, chunk, vrecv.at[direction, step]).wait()

    inner = jnp.zeros((rows, 1), F32)
    for index in range(half):
        for sub in (halves(0)[index], halves(1)[index]):
            total = part[sub, me]
            for direction in range(2):
                if depth > 1 or sub in halves(direction):
                    total = total + reduce_wait(direction, depth - 1, sub, me)
            gate, up, back = total[:, :width], total[:, width : 2 * width], total[:, 2 * width :]
            logistic = 1.0 / (1.0 + jnp.exp(-gate))
            active = gate * logistic
            hidden = (active * up).astype(BF16)
            shares[sub, me, :, :width] = hidden
            d_gate = back * up * logistic * (1.0 + gate * (1.0 - logistic))
            shares[sub, me, :, width : 2 * width] = d_gate.astype(BF16)
            shares[sub, me, :, 2 * width :] = (back * active).astype(BF16)
            for direction in range(2):
                if depth > 1 or sub in halves(direction):
                    gather_send(direction, 0, sub)
            inner = inner + jnp.sum(hidden.astype(F32) * back, axis=1, keepdims=True)
    lanes = lax.broadcasted_iota(jnp.int32, (rows, 128), 1)
    diagonal = lax.broadcasted_iota(jnp.int32, (rows, 128), 0) == lanes
    line = jnp.sum(jnp.where(diagonal, inner, 0.0), axis=0, keepdims=True)
    values[me] = jnp.broadcast_to(line, (8, 128))
    for direction in range(2):
        if depth > 1 or direction == 0:
            value_send(direction, 0)
    for step in range(1, depth + 1):
        last = step == depth
        for index in range(half):
            for sub in (halves(0)[index], halves(1)[index]):
                for direction in range(2):
                    if last and sub not in halves(direction):
                        continue
                    gather_wait(direction, step - 1, sub)
                    if not last and (step < depth - 1 or sub in halves(direction)):
                        gather_send(direction, step, sub)
        for direction in range(2):
            if last and direction == 1:
                continue
            value_wait(direction, step - 1)
            if not last and (step < depth - 1 or direction == 0):
                value_send(direction, step)
    return copies


def first_products(chips, place, toks, cots, weights, rows_of, part, table):
    rows, slots = rows_of.shape[2], toks.shape[1]
    wg, wu, wd, wg2, wu2, wd2 = weights
    width = wg.shape[1] // SUBS
    table[...] = jnp.zeros_like(table)
    row = lax.broadcasted_iota(jnp.int32, (rows, slots), 0).astype(F32)
    for path, src in enumerate((toks, cots)):
        pack = jnp.where(row == place[path], 1.0, 0.0).astype(BF16)
        for side in range(2):
            rows_of[path, side] = jnp.dot(pack, src[side], preferred_element_type=F32).astype(BF16)
    for sub in range(SUBS):
        units = slice(sub * width, (sub + 1) * width)
        gate = jnp.dot(rows_of[0, 0], wg[:, units], preferred_element_type=F32)
        gate = gate + jnp.dot(rows_of[0, 1], wg2[:, units], preferred_element_type=F32)
        up = jnp.dot(rows_of[0, 0], wu[:, units], preferred_element_type=F32)
        up = up + jnp.dot(rows_of[0, 1], wu2[:, units], preferred_element_type=F32)
        back = lax.dot_general(rows_of[1, 0], wd[units, :], NT, preferred_element_type=F32)
        back = back + lax.dot_general(rows_of[1, 1], wd2[units, :], NT, preferred_element_type=F32)
        for index, value in enumerate((gate, up, back)):
            value = value.reshape(chips, rows // chips, width)
            part[sub, :, :, index * width : (index + 1) * width] = value
            top = jnp.max(jnp.max(jnp.abs(value), axis=1), axis=1, keepdims=True)
            table[index] = jnp.maximum(table[index], top)


def gather_gates(top, nodes, rows, routes, name, hit, vback, count, gates_out):
    experts, slots = hit.shape[:2]
    lanes = lax.broadcasted_iota(jnp.int32, (experts, slots, 128), 2)
    diagonal = lax.broadcasted_iota(jnp.int32, (experts, slots, 128), 1) == lanes
    value = jnp.sum(jnp.where(diagonal, vback[:, 0:1, :], 0.0), axis=2, keepdims=True)
    inner = jnp.sum(jnp.where(hit, value, 0.0), axis=1)
    number = jnp.sum(count[:experts, :], axis=1, keepdims=True)
    inner = inner + BALANCE * 2 / (top * rows) * number
    gates = [jnp.sum(jnp.where(routes[k : k + 1, :] == name, inner, 0.0), axis=0, keepdims=True) for k in range(top)]
    gates = jnp.concatenate(gates, axis=0)
    gates_out[...] = jnp.zeros_like(gates_out)
    for i in range(nodes):
        gates_out[i, :, :rows] = gates[:, i * rows : (i + 1) * rows]


def combine(path, top, nodes, locals_, meta, src, out):
    experts, slots, wide = src.shape
    rows = out.shape[1]
    weights, routes = lay_out(meta, top, rows)
    columns = routes.shape[1]
    name, _, code = slot_codes(rows, top, routes, names_of(path, nodes, locals_))
    weight = jnp.zeros((experts, columns), F32)
    for k in range(top):
        weight = weight + jnp.where(routes[k : k + 1, :] == name, weights[k : k + 1, :], 0.0)
    place = lax.broadcasted_iota(jnp.int32, (1, slots, 1), 1).astype(F32)
    hit = code[:, None, :] == place
    rows_back = src[...].reshape(experts * slots, wide)
    high = weight.astype(BF16).astype(F32)
    total = jnp.zeros((columns, wide), F32)
    for share in (high, weight - high):
        spread_ = jnp.where(hit, share[:, None, :], 0.0).astype(BF16).reshape(experts * slots, columns)
        total = total + lax.dot_general(spread_, rows_back, (((0,), (0,)), ((), ())), preferred_element_type=F32)
    out[...] = total.astype(BF16).reshape(out.shape)
    return routes, name, hit


def main_kernel(
    chips, nodes, locals_, counts, count_sum, toks, cots, metaz, metal, wg_all, wu_all, wd_all, wg2, wu2, wd2,
    forward_home, back_home, gates_home,
    wg, wu, wd, rows_of, part, table, shares, values, got, stage, bounds, bounds_in,
    forward_out, back_out, values_out, forward_in, back_in, values_in, forward_sum, back_sum, gates_sum,
    wsem, rsend, rrecv, gsend, grecv, vsend, vrecv, tsend, trecv, bsend, brecv, lsend, lrecv, hsend, hrecv,
):
    core, ways, everyone = paths_of(nodes, locals_)
    top, rows = metaz.shape[1] // 2, forward_home.shape[1]
    load = []
    for index, (src, dst) in enumerate(((wg_all, wg), (wu_all, wu), (wd_all, wd))):
        load.append(pltpu.make_async_copy(src.at[core], dst, wsem.at[index]))
        load[-1].start()
    here, way = ring_way(chips)
    greet(everyone + way)
    mine = 2 * ways[0][0] + core
    own = counts[:, pl.ds(mine, 1), :].reshape(locals_, 128)
    place = places(nodes, locals_, own)
    for copy in load:
        copy.wait()
    first_products(chips, place, toks, cots, (wg, wu, wd, wg2, wu2, wd2), rows_of, part, table)
    ring_copies = ring_steps(
        chips, part, table, shares, values, got, stage, bounds, bounds_in,
        rsend, rrecv, gsend, grecv, vsend, vrecv, tsend, trecv,
    )
    count, slots = rows_of.shape[2], toks.shape[1]
    features, hidden = wg2.shape
    width = hidden // SUBS
    share = count // chips
    value = jnp.concatenate([upright(values[chip, 0:1, :], share) for chip in range(chips)], axis=0)
    row = lax.broadcasted_iota(jnp.int32, (count, slots), 0).astype(F32)
    value = jnp.sum(jnp.where(row == place[0], value, 0.0), axis=0, keepdims=True)
    values_out[...] = jnp.zeros_like(values_out)
    span = slots // locals_
    for relay in range(locals_):
        values_out[relay, :, :span] = jnp.broadcast_to(value[:, relay * span : (relay + 1) * span], (8, span))
    row = lax.broadcasted_iota(jnp.int32, (slots, count), 1).astype(F32)

    def kind(sub, index):
        return shares[sub, :, :, index * width : (index + 1) * width].reshape(count, width)

    copies = [[], []]
    for path, (out, dst) in enumerate(((forward_out, forward_in), (back_out, back_in))):
        unpack = jnp.where(row == upright(place[path], slots), 1.0, 0.0).astype(BF16)
        me, at, same, cross = ways[path]
        for side, (gate, up, down) in enumerate(((wg, wu, wd), (wg2, wu2, wd2))):
            total = jnp.zeros((count, features), F32)
            for sub in range(SUBS):
                units = slice(sub * width, (sub + 1) * width)
                if path == 0:
                    total = total + jnp.dot(kind(sub, 0), down[units, :], preferred_element_type=F32)
                else:
                    total = total + lax.dot_general(kind(sub, 1), gate[:, units], NT, preferred_element_type=F32)
                    total = total + lax.dot_general(kind(sub, 2), up[:, units], NT, preferred_element_type=F32)
            back = jnp.dot(unpack, total.astype(BF16), preferred_element_type=F32).astype(BF16)
            out[side] = back.reshape(out.shape[1:])
            peers = same if side == 0 else cross
            for step in list(range(1, len(at))) + [0]:
                if step == 0 and side == 0:
                    continue
                sem = (path, step, side)
                copies[path].append(
                    push(out.at[side, at[step]], dst.at[2 * me + core], bsend.at[sem], brecv.at[sem], peers[step])
                )
                if path == 0:
                    sem = (step, side)
                    line, slot = values_out.at[at[step]], values_in.at[2 * me + core]
                    copies[path].append(push(line, slot, lsend.at[sem], lrecv.at[sem], peers[step]))
        dst[2 * me + core] = out[0, me]
        if path == 0:
            values_in[2 * me + core] = values_out[me]

    homeward = []
    for path, (meta, src, out, dst) in enumerate(
        ((metaz, forward_in, forward_sum, forward_home), (metal, back_in, back_sum, back_home))
    ):
        for copy in copies[path]:
            copy.wait_recv()
        routes, name, hit = combine(path, top, nodes, locals_, meta, src, out)
        me, at, peers, _ = ways[1 - path]
        for step in range(1, len(at)):
            sem = (step, path)
            homeward.append(push(out.at[at[step]], dst.at[step], hsend.at[sem], hrecv.at[sem], peers[step]))
        dst[0] = out[me]
        if path == 0:
            gather_gates(top, nodes, rows, routes, name, hit, values_in, count_sum, gates_sum)
            for step in range(1, len(at)):
                sem = (step, 2)
                homeward.append(
                    push(gates_sum.at[at[step]], gates_home.at[step], hsend.at[sem], hrecv.at[sem], peers[step])
                )
            gates_home[0] = gates_sum[me]
    for copy in homeward:
        copy.wait()
    for copy in copies[0] + copies[1] + ring_copies:
        copy.wait_send()


def main(chips, nodes, locals_, count, ident, counts, count_sum, toks, cots, metaz, metal, rows, wg, wu, wd, wg2, wu2, wd2):
    top = metaz.shape[1] // 2
    _, slots, features = toks.shape
    wide = 3 * (wg.shape[2] // SUBS)
    depth = chips // 2
    share = count // chips
    most = max(nodes, locals_)
    table = (3, chips, 128)
    forward = (2, locals_, nodes * CAP, features)
    back = (2, nodes, locals_ * CAP, features)
    homes = [((nodes, rows, features), BF16), ((locals_, rows, features), BF16), ((nodes, top, 128), F32)]
    dma = pltpu.SemaphoreType.DMA
    return pl.pallas_call(
        functools.partial(main_kernel, chips, nodes, locals_),
        out_shape=[jax.ShapeDtypeStruct(*one) for one in homes],
        in_specs=[VMEM] * 6 + [ANY] * 3 + [VMEM] * 3,
        out_specs=[VMEM] * 3,
        scratch_shapes=[pltpu.VMEM(w.shape, BF16) for w in (wg2, wu2, wd2)]
        + [
            pltpu.VMEM((2, 2, count, features), BF16),
            pltpu.VMEM((SUBS, chips, share, wide), F32),
            pltpu.VMEM(table, F32),
            pltpu.VMEM((SUBS, chips, share, wide), BF16),
            pltpu.VMEM((chips, 8, 128), F32),
            pltpu.VMEM((2, depth, SUBS, share, wide), jnp.int16),
            pltpu.VMEM((2, depth, SUBS, share, wide), jnp.int16),
            pltpu.VMEM((2, depth) + table, F32),
            pltpu.VMEM((2, depth) + table, F32),
            pltpu.VMEM(forward, BF16),
            pltpu.VMEM(back, BF16),
            pltpu.VMEM((locals_, 8, 128), F32),
            pltpu.VMEM((2 * locals_,) + forward[2:], BF16),
            pltpu.VMEM((2 * nodes,) + back[2:], BF16),
            pltpu.VMEM((2 * locals_, 8, 128), F32),
        ]
        + [pltpu.VMEM(*one) for one in homes]
        + [dma((3,))]
        + [dma((2, depth, SUBS))] * 4
        + [dma((2, depth))] * 4
        + [dma((2, most, 2))] * 2
        + [dma((locals_, 2))] * 2
        + [dma((most, 3))] * 2,
        compiler_params=pltpu.CompilerParams(collective_id=ident, has_side_effects=True, vmem_limit_bytes=LIMIT),
    )(counts, count_sum, toks, cots, metaz, metal, wg, wu, wd, wg2, wu2, wd2)


def total_kernel(forward, back, gates, mixed, grads, gates_out):
    mixed[...] = jnp.sum(forward[...].astype(F32), axis=0).astype(BF16)
    grads[...] = jnp.sum(back[...].astype(F32), axis=0).astype(BF16)
    gates_out[...] = jnp.sum(gates[...], axis=0)[:, : gates_out.shape[1]]


def total(forward, back, gates):
    _, rows, features = forward.shape
    half = jax.ShapeDtypeStruct((rows, features), BF16)
    return pl.pallas_call(
        total_kernel,
        out_shape=[half, half, jax.ShapeDtypeStruct((gates.shape[1], rows), F32)],
        in_specs=[VMEM] * 3,
        out_specs=[VMEM] * 3,
        compiler_params=pltpu.CompilerParams(vmem_limit_bytes=LIMIT),
    )(forward, back, gates)


def body(chips, nodes, locals_, tokens, cotangent, routes, gate_weights, w_gate, w_up, w_down):
    rows, features = tokens.shape
    slots = nodes * locals_ * CAP
    toks, cots, counts, count_sum, metaz, metal, *swapped = front(
        nodes, locals_, tokens, cotangent, gate_weights.T, routes.T, w_gate, w_up, w_down
    )
    toks, cots = toks.reshape(2, slots, features), cots.reshape(2, slots, features)

    def sized(count, ident):
        def call(*operands):
            return main(chips, nodes, locals_, count, ident, *operands[:6], rows, *operands[6:])

        return call

    crowded = jnp.max(count_sum[2 * locals_ :, :]) > USUAL * chips
    operands = (counts, count_sum, toks, cots, metaz, metal, w_gate, w_up, w_down, *swapped)
    sums = lax.cond(crowded, sized(slots, 2), sized(USUAL * chips, 1), *operands)
    mixed, grads, gates = total(*sums)
    return mixed, grads, gates.T


def solution(mesh):
    chips, nodes, locals_ = mesh.shape["dp"] // 2, mesh.shape["node"], mesh.shape["local"]
    placed = (
        P(("node", "local"), "dp"),
        P(("node", "local"), "dp"),
        P(("node", "local"), None),
        P(("node", "local"), None),
        P(("node", "local"), "dp", None),
        P(("node", "local"), "dp", None),
        P(("node", "local"), None, "dp"),
    )
    return jax.shard_map(
        functools.partial(body, chips, nodes, locals_),
        mesh=mesh,
        in_specs=placed,
        out_specs=(
            P(("node", "local"), "dp"),
            P(("node", "local"), "dp"),
            P(("node", "local"), None),
        ),
        check_vma=False,
    )
```

```python
import functools

import jax
import jax.numpy as jnp
from jax import lax
from jax.experimental import pallas as pl
from jax.experimental.pallas import tpu as pltpu
from jax.sharding import PartitionSpec as P

BALANCE = 2.0
CAP = 6
USUAL = 32
SUBS = 4
STEPS = 32766.0
MESH = pl.DeviceIdType.MESH
F32, BF16 = jnp.float32, jnp.bfloat16
VMEM = pl.BlockSpec(memory_space=pltpu.VMEM)
ANY = pl.BlockSpec(memory_space=pl.ANY)
LIMIT = 56 * 1024 * 1024


def hail(peers):
    barrier = pltpu.get_barrier_semaphore()
    for peer in peers:
        pl.semaphore_signal(barrier, inc=1, device_id=peer, device_id_type=MESH)


def await_all(peers):
    pl.semaphore_wait(pltpu.get_barrier_semaphore(), len(peers))


def push(src, dst, send, recv, peer):
    copy = pltpu.make_async_remote_copy(
        src_ref=src, dst_ref=dst, send_sem=send, recv_sem=recv, device_id=peer, device_id_type=MESH
    )
    copy.start()
    return copy


def other_core():
    core = lax.rem(lax.axis_index("dp"), 2)
    return core, lax.axis_index("dp") + 1 - 2 * core


def upright(line, rows):
    lanes = lax.broadcasted_iota(jnp.int32, (rows, line.shape[-1]), 1)
    diagonal = lax.broadcasted_iota(jnp.int32, (rows, line.shape[-1]), 0) == lanes
    return jnp.sum(jnp.where(diagonal, line, 0.0), axis=1, keepdims=True)


def lying(column, lanes):
    rows = column.shape[0]
    lane = lax.broadcasted_iota(jnp.int32, (rows, lanes), 1)
    diagonal = lax.broadcasted_iota(jnp.int32, (rows, lanes), 0) == lane
    return jnp.sum(jnp.where(diagonal, column, 0.0), axis=0, keepdims=True)


def ring_of(axis, size):
    me = lax.axis_index(axis)
    return me, [lax.rem(me + step, size) for step in range(size)]


def names_of(path, nodes, locals_):
    if path == 0:
        return lax.broadcasted_iota(jnp.int32, (2 * locals_, 1), 0) + 2 * locals_ * lax.axis_index("node")
    order = lax.broadcasted_iota(jnp.int32, (2 * nodes, 1), 0)
    return (order >> 1) * (2 * locals_) + (order & 1) + 2 * lax.axis_index("local")


def slot_codes(rows, top, routes, names):
    columns = routes.shape[1]
    experts = names.shape[0]
    name = jnp.broadcast_to(names.astype(F32), (experts, columns))
    chosen = jnp.zeros((experts, columns), F32)
    for k in range(top):
        chosen = chosen + jnp.where(routes[k : k + 1, :] == name, 1.0, 0.0)
    scale = -(-32768 // rows)
    earlier = lax.broadcasted_iota(jnp.int32, (columns, columns), 0)
    later = lax.broadcasted_iota(jnp.int32, (columns, columns), 1)
    block_row = (earlier * scale) >> 15
    block_col = (later * scale) >> 15
    before = jnp.where((block_row == block_col) & (earlier < later), 1.0, 0.0).astype(BF16)
    rank = jnp.dot(chosen.astype(BF16), before, preferred_element_type=F32)
    block = (lax.broadcasted_iota(jnp.int32, (experts, columns), 1) * scale >> 15).astype(F32)
    code = jnp.where(chosen > 0.0, block * CAP + rank, -1.0)
    return name, chosen, code


def lay_out(meta, top, rows):
    blocks = meta.shape[0]
    weights = jnp.concatenate([meta[i, :top, :rows] for i in range(blocks)], axis=1)
    routes = jnp.concatenate([meta[i, :top, 64 : 64 + rows] for i in range(blocks)], axis=1)
    return weights, routes


def paths_of(nodes, locals_):
    core, twin = other_core()
    ways = []
    for axis, size in (("local", locals_), ("node", nodes)):
        me, at = ring_of(axis, size)
        ways.append((me, at, [{axis: one} for one in at], [{axis: one, "dp": twin} for one in at]))
    peers = ways[0][2][1:] + ways[1][2][1:] + ways[0][3] + ways[1][3][1:]
    return core, ways, peers


def pick_rows(path, top, nodes, locals_, rows, meta, experts, slots, count):
    _, routes = lay_out(meta, top, rows)
    columns = routes.shape[1]
    _, chosen, code = slot_codes(rows, top, routes, names_of(path, nodes, locals_))
    place = lax.broadcasted_iota(jnp.int32, (1, slots, 1), 1).astype(F32)
    pick = jnp.where(code[:, None, :] == place, 1.0, 0.0).astype(BF16).reshape(experts * slots, columns)
    if path == 0:
        block = (lax.broadcasted_iota(jnp.int32, (columns, 128), 0) * -(-32768 // rows)) >> 15
        by_block = jnp.where(block == lax.broadcasted_iota(jnp.int32, (columns, 128), 1), 1.0, 0.0).astype(BF16)
        count[:experts, :] = jnp.dot(chosen.astype(BF16), by_block, preferred_element_type=F32)
        total = 2 * nodes * locals_
        name = lax.broadcasted_iota(jnp.int32, (total, columns), 0).astype(F32)
        hits = jnp.zeros((total, columns), F32)
        for k in range(top):
            hits = hits + jnp.where(routes[k : k + 1, :] == name, 1.0, 0.0)
        count[experts:, :] = jnp.broadcast_to(lying(jnp.sum(hits, axis=1, keepdims=True), 128), (8, 128))
    return pick


def front_steps(
    nodes, locals_, ways, core, tok, cot, gates, routes, tok_in, cot_in, counts, count_sum, metaz, metal, swap,
    meta, tokz, cotl, tok_out, cot_out, count, send, recv, ssend, srecv, csend, crecv,
):
    place, _, side, _ = ways[0]
    node, _, far, _ = ways[1]
    top, rows = gates.shape
    blocks = [[], []]
    for step in range(1, max(nodes, locals_)):
        for path, (peers, me, arrays) in enumerate(
            ((far, node, ((meta, metaz), (tok, tokz))), (side, place, ((meta, metal), (cot, cotl))))
        ):
            if step < len(peers):
                for index, (src, dst) in enumerate(arrays):
                    at = (path, step - 1, index)
                    blocks[index].append((path, push(src, dst.at[me], send.at[at], recv.at[at], peers[step])))
    swap()
    tokz[node] = tok[...]
    cotl[place] = cot[...]
    metaz[node] = meta[...]
    metal[place] = meta[...]
    picks, numbers, copies = [], [], [[], []]
    for path, (met, out) in enumerate(((metaz, tok_out), (metal, cot_out))):
        for which, copy in blocks[0]:
            if which == path:
                copy.wait_recv()
        picks.append(pick_rows(path, top, nodes, locals_, rows, met, out.shape[0], out.shape[1], count))
        if path == 0:
            for step in range(1, locals_):
                sem = step - 1
                numbers.append(push(count, counts.at[place], csend.at[sem], crecv.at[sem], side[step]))
            counts[place] = count[...]
    for path, (src, out, dst) in enumerate(((tokz, tok_out, tok_in), (cotl, cot_out, cot_in))):
        for which, copy in blocks[1]:
            if which == path:
                copy.wait_recv()
        picked = jnp.dot(picks[path], src[...].reshape(-1, src.shape[2]), preferred_element_type=F32)
        out[...] = picked.astype(BF16).reshape(out.shape)
        me, at, same, cross = ways[path]
        for step in list(range(1, len(at))) + [0]:
            for distant, peers in enumerate((same, cross)):
                if step == 0 and distant == 0:
                    continue
                expert = 2 * at[step] + (core if distant == 0 else 1 - core)
                sem = (path, step, distant)
                copies[path].append(push(out.at[expert], dst.at[distant, me], ssend.at[sem], srecv.at[sem], peers[step]))
        dst[0, me] = out[2 * me + core]
    return numbers, copies[0], copies[1], [copy for _, copy in blocks[0] + blocks[1]]


def fill_meta(gates, routes, meta):
    top, rows = gates.shape
    meta[...] = jnp.zeros_like(meta)
    meta[:, :rows] = gates[...]
    meta[:, 64 : 64 + rows] = routes[...].astype(F32)


def front_kernel(
    nodes, locals_, tok, cot, gates, routes, wg, wu, wd,
    tok_in, cot_in, counts, count_sum, metaz, metal, wg2, wu2, wd2, wsend, wrecv, meta, *scratch,
):
    core, ways, everyone = paths_of(nodes, locals_)
    _, twin = other_core()
    fill_meta(gates, routes, meta)
    hail(everyone)
    await_all(everyone)
    copies = []

    def swap():
        for index, (src, dst) in enumerate(((wg, wg2), (wu, wu2), (wd, wd2))):
            copies.append(push(src.at[1 - core], dst, wsend.at[index], wrecv.at[index], {"dp": twin}))

    numbers, toks, cots, blocks = front_steps(
        nodes, locals_, ways, core, tok, cot, gates, routes, tok_in, cot_in, counts, count_sum, metaz, metal, swap,
        meta, *scratch,
    )
    for copy in copies + numbers + toks + cots:
        copy.wait()
    for copy in blocks:
        copy.wait_send()
    count_sum[...] = jnp.sum(counts[...], axis=0)


def front_shapes(nodes, locals_, features, top):
    meta, count = (top, 128), (2 * locals_ + 8, 128)
    return [
        ((2, locals_, nodes * CAP, features), BF16),
        ((2, nodes, locals_ * CAP, features), BF16),
        ((locals_,) + count, F32),
        (count, F32),
        ((nodes,) + meta, F32),
        ((locals_,) + meta, F32),
    ]


def front_scratch(nodes, locals_, rows, features, top):
    most = max(nodes, locals_)
    dma = pltpu.SemaphoreType.DMA
    return (
        [
            pltpu.VMEM((top, 128), F32),
            pltpu.VMEM((nodes, rows, features), BF16),
            pltpu.VMEM((locals_, rows, features), BF16),
            pltpu.VMEM((2 * locals_, nodes * CAP, features), BF16),
            pltpu.VMEM((2 * nodes, locals_ * CAP, features), BF16),
            pltpu.VMEM((2 * locals_ + 8, 128), F32),
        ]
        + [dma((2, most, 2))] * 4
        + [dma((locals_,))] * 2
    )


def front(nodes, locals_, tok, cot, gates, routes, wg, wu, wd):
    rows, features = tok.shape
    top = gates.shape[0]
    return pl.pallas_call(
        functools.partial(front_kernel, nodes, locals_),
        out_shape=[jax.ShapeDtypeStruct(*one) for one in front_shapes(nodes, locals_, features, top)]
        + [jax.ShapeDtypeStruct(a.shape[1:], a.dtype) for a in (wg, wu, wd)],
        in_specs=[VMEM] * 4 + [ANY] * 3,
        out_specs=[VMEM] * 6 + [ANY] * 3,
        scratch_shapes=[pltpu.SemaphoreType.DMA((3,))] * 2 + front_scratch(nodes, locals_, rows, features, top),
        compiler_params=pltpu.CompilerParams(collective_id=1, has_side_effects=True, vmem_limit_bytes=LIMIT),
    )(tok, cot, gates, routes, wg, wu, wd)


NT = (((1,), (1,)), ((), ()))


def places(nodes, locals_, counts):
    slots = nodes * locals_ * CAP
    index = lax.broadcasted_iota(jnp.int32, (locals_, slots), 1).astype(F32)
    axis = lax.broadcasted_iota(jnp.int32, (locals_, slots), 0).astype(F32)
    lane = lax.broadcasted_iota(jnp.int32, (128, slots), 0).astype(F32)
    earlier = lax.broadcasted_iota(jnp.int32, (slots, slots), 0).astype(F32)
    rows, valid = [], None
    for path, inner in enumerate((nodes, locals_)):
        major = jnp.floor((index + 0.5) * (1.0 / (CAP * inner)))
        within = index - major * (CAP * inner)
        minor = jnp.floor((within + 0.5) * (1.0 / CAP))
        rank = within - minor * CAP
        of_node, of_local = (minor, major) if path == 0 else (major, minor)
        by_node = jnp.where(lane == of_node[:1, :], 1.0, 0.0).astype(BF16)
        count = jnp.dot(counts.astype(BF16), by_node, preferred_element_type=F32)
        count = jnp.sum(jnp.where(axis == of_local, count, 0.0), axis=0, keepdims=True)
        filled = rank[:1, :] < count
        if path == 0:
            valid = jnp.broadcast_to(jnp.where(filled, 1.0, 0.0), (8, slots)).astype(BF16)
        first_path = of_local[:1, :] * (CAP * nodes) + of_node[:1, :] * CAP + rank[:1, :]
        before = jnp.where(earlier < first_path, 1.0, 0.0).astype(BF16)
        row = jnp.dot(valid, before, preferred_element_type=F32)[:1, :]
        rows.append(jnp.where(filled, row, -1.0))
    return rows


def ring_way(chips):
    core, _ = other_core()
    me = (lax.axis_index("dp") - core) // 2
    return me, [{"dp": 2 * lax.rem(me + step + chips, chips) + core} for step in (1, -1)]


def ring_steps(
    chips, early, late, ready, part, table, shares, values, got, stage, bounds, bounds_in,
    rsend, rrecv, gsend, grecv, vsend, vrecv, tsend, trecv,
):
    me, way = ring_way(chips)
    depth = chips // 2
    half = SUBS // 2
    width = part.shape[3] // 3
    rows = part.shape[2]

    def chip(offset):
        return lax.rem(me + offset + 2 * chips, chips)

    sign = (1, -1)

    def halves(direction):
        return range(half) if direction == 0 else range(half, SUBS)

    copies = []

    def bound(ref, chunk):
        line = ref[pl.ds(chunk, 1), :]
        kinds = [jnp.broadcast_to(line[:, 32 * index : 32 * index + 1], (1, width)) for index in range(3)]
        return jnp.concatenate(kinds, axis=1)

    def reduce_send(direction, step, sub, total, chunk):
        at = (direction, step, sub)
        limit = bound(bounds.at[direction, step], chunk)
        inverse = jnp.where(limit > 1e-30, STEPS / jnp.maximum(limit, 1e-30), 0.0)
        stage[at] = jnp.round(total * inverse).astype(jnp.int32).astype(jnp.int16)
        copies.append(push(stage.at[at], got.at[at], rsend.at[at], rrecv.at[at], way[direction]))

    def reduce_wait(direction, step, sub, chunk):
        at = (direction, step, sub)
        pltpu.make_async_copy(got.at[at], got.at[at], rrecv.at[at]).wait()
        limit = bound(bounds_in.at[direction, step], chunk)
        return got[at].astype(jnp.int32).astype(F32) * (limit * (1.0 / STEPS))

    def bound_send(direction, step):
        at = (direction, step)
        copies.append(push(bounds.at[at], bounds_in.at[at], tsend.at[at], trecv.at[at], way[direction]))

    def bound_wait(direction, step):
        at = (direction, step)
        pltpu.make_async_copy(bounds_in.at[at], bounds_in.at[at], trecv.at[at]).wait()

    for direction in range(2):
        bounds[direction, 0] = table[...]
        bound_send(direction, 0)
    for index in range(half):
        for direction in range(2):
            sub = halves(direction)[index]
            chunk = chip(sign[direction] * depth)
            reduce_send(direction, 0, sub, part[sub, chunk], chunk)
    early()
    for step in range(1, depth):
        for direction in range(2):
            bound_wait(direction, step - 1)
            bounds[direction, step] = table[...] + bounds_in[direction, step - 1]
            bound_send(direction, step)
        for index in range(half):
            for direction in range(2):
                if step == 1:
                    sub = halves(1 - direction)[index]
                    chunk = chip(sign[direction] * (depth - 1))
                    reduce_send(direction, 1, sub, part[sub, chunk], chunk)
        for sub in range(SUBS):
            for direction in range(2):
                if step == 1 and sub not in halves(direction):
                    continue
                chunk = chip(sign[direction] * (depth - step))
                total = part[sub, chunk] + reduce_wait(direction, step - 1, sub, chunk)
                reduce_send(direction, step, sub, total, chunk)
    for direction in range(2):
        bound_wait(direction, depth - 1)

    def gather_send(direction, step, sub):
        chunk = shares.at[sub, chip(-sign[direction] * step)]
        at = (direction, step, sub)
        copies.append(push(chunk, chunk, gsend.at[at], grecv.at[at], way[direction]))

    def gather_wait(direction, step, sub):
        chunk = shares.at[sub, chip(-sign[direction] * (step + 1))]
        pltpu.make_async_copy(chunk, chunk, grecv.at[direction, step, sub]).wait()

    def value_send(direction, step):
        chunk = values.at[chip(-sign[direction] * step)]
        at = (direction, step)
        copies.append(push(chunk, chunk, vsend.at[at], vrecv.at[at], way[direction]))

    def value_wait(direction, step):
        chunk = values.at[chip(-sign[direction] * (step + 1))]
        pltpu.make_async_copy(chunk, chunk, vrecv.at[direction, step]).wait()

    inner = jnp.zeros((rows, 1), F32)
    for index in range(half):
        for sub in (halves(0)[index], halves(1)[index]):
            total = part[sub, me]
            for direction in range(2):
                if depth > 1 or sub in halves(direction):
                    total = total + reduce_wait(direction, depth - 1, sub, me)
            gate, up, back = total[:, :width], total[:, width : 2 * width], total[:, 2 * width :]
            logistic = 1.0 / (1.0 + jnp.exp(-gate))
            active = gate * logistic
            hidden = (active * up).astype(BF16)
            shares[sub, me, :, :width] = hidden
            d_gate = back * up * logistic * (1.0 + gate * (1.0 - logistic))
            shares[sub, me, :, width : 2 * width] = d_gate.astype(BF16)
            shares[sub, me, :, 2 * width :] = (back * active).astype(BF16)
            for direction in range(2):
                if depth > 1 or sub in halves(direction):
                    gather_send(direction, 0, sub)
            inner = inner + jnp.sum(hidden.astype(F32) * back, axis=1, keepdims=True)
    lanes = lax.broadcasted_iota(jnp.int32, (rows, 128), 1)
    diagonal = lax.broadcasted_iota(jnp.int32, (rows, 128), 0) == lanes
    line = jnp.sum(jnp.where(diagonal, inner, 0.0), axis=0, keepdims=True)
    values[me] = line
    for direction in range(2):
        if depth > 1 or direction == 0:
            value_send(direction, 0)
    for step in range(1, depth + 1):
        last = step == depth
        for direction in range(2):
            if last and direction == 1:
                continue
            value_wait(direction, step - 1)
            if not last and (step < depth - 1 or direction == 0):
                value_send(direction, step)
        if last:
            late()
        for index in range(half):
            for sub in (halves(0)[index], halves(1)[index]):
                for direction in range(2):
                    if last and sub not in halves(direction):
                        continue
                    gather_wait(direction, step - 1, sub)
                    if not last and (step < depth - 1 or sub in halves(direction)):
                        gather_send(direction, step, sub)
                if last:
                    ready(sub)
    return copies


def pack_rows(place, src, dst):
    _, rows, features = dst.shape
    row = lax.broadcasted_iota(jnp.int32, (rows, place.shape[1]), 0).astype(F32)
    pack = jnp.where(row == place, 1.0, 0.0).astype(BF16)
    for side in range(2):
        slots = src[side].reshape(-1, features)
        dst[side] = jnp.dot(pack, slots, preferred_element_type=F32).astype(BF16)


def first_products(chips, kinds, rows_of, part, table):
    rows = rows_of.shape[1]
    width = part.shape[3] // 3
    lane_kind = lax.broadcasted_iota(jnp.int32, (chips, 128), 1) >> 5
    for sub in range(SUBS):
        units = slice(sub * width, (sub + 1) * width)
        for index, (own, twin) in kinds:
            if index < 2:
                value = jnp.dot(rows_of[0], own[:, units], preferred_element_type=F32)
                value = value + jnp.dot(rows_of[1], twin[:, units], preferred_element_type=F32)
            else:
                value = lax.dot_general(rows_of[0], own[units, :], NT, preferred_element_type=F32)
                value = value + lax.dot_general(rows_of[1], twin[units, :], NT, preferred_element_type=F32)
            value = value.reshape(chips, rows // chips, width)
            part[sub, :, :, index * width : (index + 1) * width] = value
            top = jnp.max(jnp.max(jnp.abs(value), axis=1), axis=1, keepdims=True)
            table[...] = jnp.maximum(table[...], jnp.where(lane_kind == index, top, 0.0))


def gather_gates(top, nodes, rows, routes, name, hit, vback, count, gates_out):
    experts, slots = hit.shape[:2]
    lanes = lax.broadcasted_iota(jnp.int32, (experts, slots, 128), 2)
    diagonal = lax.broadcasted_iota(jnp.int32, (experts, slots, 128), 1) == lanes
    value = jnp.sum(jnp.where(diagonal, vback[:, 0:1, :], 0.0), axis=2, keepdims=True)
    inner = jnp.sum(jnp.where(hit, value, 0.0), axis=1)
    number = jnp.sum(count[:experts, :], axis=1, keepdims=True)
    inner = inner + BALANCE * 2 / (top * rows) * number
    gates = [jnp.sum(jnp.where(routes[k : k + 1, :] == name, inner, 0.0), axis=0, keepdims=True) for k in range(top)]
    gates = jnp.concatenate(gates, axis=0)
    gates_out[...] = jnp.zeros_like(gates_out)
    for i in range(nodes):
        gates_out[i, :, :rows] = gates[:, i * rows : (i + 1) * rows]


def weigh(path, top, nodes, locals_, rows, meta, experts, slots):
    weights, routes = lay_out(meta, top, rows)
    columns = routes.shape[1]
    name, _, code = slot_codes(rows, top, routes, names_of(path, nodes, locals_))
    weight = jnp.zeros((experts, columns), F32)
    for k in range(top):
        weight = weight + jnp.where(routes[k : k + 1, :] == name, weights[k : k + 1, :], 0.0)
    place = lax.broadcasted_iota(jnp.int32, (1, slots, 1), 1).astype(F32)
    hit = code[:, None, :] == place
    high = weight.astype(BF16).astype(F32)
    shares = [
        jnp.where(hit, share[:, None, :], 0.0).astype(BF16).reshape(experts * slots, columns).T
        for share in (high, weight - high)
    ]
    return routes, name, hit, shares


def main_steps(
    chips, nodes, locals_, ways, core, ready_counts, ready_weights, ready_toks, ready_cots, ready_peers,
    counts, count_sum, toks, cots, metaz, metal, forward_home, back_home, gates_home,
    wg, wu, wd, wg2, wu2, wd2, unpack, sums, rows_of, part, table, shares, values, got, stage, bounds, bounds_in,
    forward_out, back_out, values_out, forward_in, back_in, values_in, forward_sum, back_sum, gates_sum,
    rsend, rrecv, gsend, grecv, vsend, vrecv, tsend, trecv, bsend, brecv, lsend, lrecv, hsend, hrecv,
):
    top, rows = metaz.shape[1], forward_home.shape[1]
    count = rows_of.shape[2]
    slots = nodes * locals_ * CAP
    features, hidden = wg2.shape
    width = hidden // SUBS
    share = count // chips
    span = slots // locals_
    table[...] = jnp.zeros_like(table)
    ready_counts()
    mine = 2 * ways[0][0] + core
    own = counts[:, pl.ds(mine, 1), :].reshape(locals_, 128)
    place = places(nodes, locals_, own)
    ready_weights()
    ready_toks()
    pack_rows(place[0], toks, rows_of.at[0])
    first_products(chips, ((0, (wg, wg2)), (1, (wu, wu2))), rows_of.at[0], part, table)
    ready_cots()
    pack_rows(place[1], cots, rows_of.at[1])
    first_products(chips, ((2, (wd, wd2)),), rows_of.at[1], part, table)
    ready_peers()
    value_copies = []

    def early():
        row = lax.broadcasted_iota(jnp.int32, (slots, count), 1).astype(F32)
        for path in range(2):
            unpack[path] = jnp.where(row == upright(place[path], slots), 1.0, 0.0).astype(BF16)

    def late():
        value = jnp.concatenate([upright(values[chip, 0:1, :], share) for chip in range(chips)], axis=0)
        row = lax.broadcasted_iota(jnp.int32, (count, slots), 0).astype(F32)
        value = jnp.sum(jnp.where(row == place[0], value, 0.0), axis=0, keepdims=True)
        values_out[...] = jnp.zeros_like(values_out)
        for relay in range(locals_):
            values_out[relay, :, :span] = value[:, relay * span : (relay + 1) * span]
        me, at, same, cross = ways[0]
        for step in range(locals_):
            for side, peers in enumerate((same, cross)):
                if step == 0 and side == 0:
                    continue
                sem = (step, side)
                line, slot = values_out.at[at[step]], values_in.at[2 * me + core]
                value_copies.append(push(line, slot, lsend.at[sem], lrecv.at[sem], peers[step]))
        values_in[2 * me + core] = values_out[me]
        sums[...] = jnp.zeros_like(sums)

    def kind(sub, index):
        return shares[sub, :, :, index * width : (index + 1) * width].reshape(count, width)

    def ready(sub):
        units = slice(sub * width, (sub + 1) * width)
        for side, (gate, up, down) in enumerate(((wg, wu, wd), (wg2, wu2, wd2))):
            sums[0, side] += jnp.dot(kind(sub, 0), down[units, :], preferred_element_type=F32)
            back = lax.dot_general(kind(sub, 1), gate[:, units], NT, preferred_element_type=F32)
            back = back + lax.dot_general(kind(sub, 2), up[:, units], NT, preferred_element_type=F32)
            sums[1, side] += back

    ring_copies = ring_steps(
        chips, early, late, ready, part, table, shares, values, got, stage, bounds, bounds_in,
        rsend, rrecv, gsend, grecv, vsend, vrecv, tsend, trecv,
    )
    copies = [[], []]
    for path, (out, dst) in enumerate(((forward_out, forward_in), (back_out, back_in))):
        me, at, same, cross = ways[path]
        for side in range(2):
            back = jnp.dot(unpack[path], sums[path, side].astype(BF16), preferred_element_type=F32).astype(BF16)
            out[side] = back.reshape(out.shape[1:])
            peers = same if side == 0 else cross
            for step in list(range(1, len(at))) + [0]:
                if step == 0 and side == 0:
                    continue
                sem = (path, step, side)
                copies[path].append(
                    push(out.at[side, at[step]], dst.at[2 * me + core], bsend.at[sem], brecv.at[sem], peers[step])
                )
        dst[2 * me + core] = out[0, me]

    weighed = [
        weigh(path, top, nodes, locals_, rows, meta, src.shape[0], src.shape[1])
        for path, (meta, src) in enumerate(((metaz, forward_in), (metal, back_in)))
    ]
    homeward = []
    for path, (src, out, dst) in enumerate(((forward_in, forward_sum, forward_home), (back_in, back_sum, back_home))):
        routes, name, hit, parts = weighed[path]
        for copy in copies[path]:
            copy.wait_recv()
        if path == 0:
            for copy in value_copies:
                copy.wait_recv()
        rows_back = src[...].reshape(-1, src.shape[2])
        total = jnp.dot(parts[0], rows_back, preferred_element_type=F32)
        total = total + jnp.dot(parts[1], rows_back, preferred_element_type=F32)
        out[...] = total.astype(BF16).reshape(out.shape)
        me, at, peers, _ = ways[1 - path]
        for step in range(1, len(at)):
            sem = (step, path)
            homeward.append(push(out.at[at[step]], dst.at[step], hsend.at[sem], hrecv.at[sem], peers[step]))
        dst[0] = out[me]
        if path == 0:
            gather_gates(top, nodes, rows, routes, name, hit, values_in, count_sum, gates_sum)
            for step in range(1, len(at)):
                sem = (step, 2)
                homeward.append(
                    push(gates_sum.at[at[step]], gates_home.at[step], hsend.at[sem], hrecv.at[sem], peers[step])
                )
            gates_home[0] = gates_sum[me]
    for copy in homeward:
        copy.wait()
    for copy in copies[0] + copies[1] + value_copies + ring_copies:
        copy.wait_send()


def main_shapes(nodes, locals_, rows, features, top):
    return [((nodes, rows, features), BF16), ((locals_, rows, features), BF16), ((nodes, top, 128), F32)]


def main_scratch(chips, nodes, locals_, count, rows, features, hidden, top):
    wide = 3 * (hidden // SUBS)
    depth = chips // 2
    share = count // chips
    most = max(nodes, locals_)
    forward, back, _, _, _, _ = (shape for shape, _ in front_shapes(nodes, locals_, features, top))
    dma = pltpu.SemaphoreType.DMA
    return (
        [pltpu.VMEM(shape, BF16) for shape in ((features, hidden), (features, hidden), (hidden, features)) * 2]
        + [
            pltpu.VMEM((2, nodes * locals_ * CAP, count), BF16),
            pltpu.VMEM((2, 2, count, features), F32),
            pltpu.VMEM((2, 2, count, features), BF16),
            pltpu.VMEM((SUBS, chips, share, wide), F32),
            pltpu.VMEM((chips, 128), F32),
            pltpu.VMEM((SUBS, chips, share, wide), BF16),
            pltpu.VMEM((chips, 1, 128), F32),
            pltpu.VMEM((2, depth, SUBS, share, wide), jnp.int16),
            pltpu.VMEM((2, depth, SUBS, share, wide), jnp.int16),
            pltpu.VMEM((2, depth, chips, 128), F32),
            pltpu.VMEM((2, depth, chips, 128), F32),
            pltpu.VMEM(forward, BF16),
            pltpu.VMEM(back, BF16),
            pltpu.VMEM((locals_, 1, 128), F32),
            pltpu.VMEM((2 * locals_,) + forward[2:], BF16),
            pltpu.VMEM((2 * nodes,) + back[2:], BF16),
            pltpu.VMEM((2 * locals_, 1, 128), F32),
        ]
        + [pltpu.VMEM(*one) for one in main_shapes(nodes, locals_, rows, features, top)]
        + [dma((2, depth, SUBS))] * 4
        + [dma((2, depth))] * 4
        + [dma((2, most, 2))] * 2
        + [dma((locals_, 2))] * 2
        + [dma((most, 3))] * 2
    )


def main_kernel(
    chips, nodes, locals_, counts, count_sum, toks, cots, metaz, metal, wg_own, wu_own, wd_own, wg_twin, wu_twin, wd_twin,
    forward_home, back_home, gates_home, wsem, wg, wu, wd, wg2, wu2, wd2, *scratch,
):
    core, ways, everyone = paths_of(nodes, locals_)
    _, way = ring_way(chips)
    hail(everyone + way)
    sources = (wg_own.at[core], wu_own.at[core], wd_own.at[core], wg_twin, wu_twin, wd_twin)
    load = []
    for index, (src, dst) in enumerate(zip(sources, (wg, wu, wd, wg2, wu2, wd2))):
        load.append(pltpu.make_async_copy(src, dst, wsem.at[index]))
        load[-1].start()

    def nothing():
        pass

    def ready_weights():
        for copy in load:
            copy.wait()

    main_steps(
        chips, nodes, locals_, ways, core, nothing, ready_weights, nothing, nothing, lambda: await_all(everyone + way),
        counts, count_sum, toks, cots, metaz, metal, forward_home, back_home, gates_home,
        wg, wu, wd, wg2, wu2, wd2, *scratch,
    )


def main(chips, nodes, locals_, count, counts, count_sum, toks, cots, metaz, metal, rows, wg, wu, wd, wg2, wu2, wd2):
    top = metaz.shape[1]
    features, hidden = wg2.shape
    return pl.pallas_call(
        functools.partial(main_kernel, chips, nodes, locals_),
        out_shape=[jax.ShapeDtypeStruct(*one) for one in main_shapes(nodes, locals_, rows, features, top)],
        in_specs=[VMEM] * 6 + [ANY] * 6,
        out_specs=[VMEM] * 3,
        scratch_shapes=[pltpu.SemaphoreType.DMA((6,))]
        + main_scratch(chips, nodes, locals_, count, rows, features, hidden, top),
        compiler_params=pltpu.CompilerParams(collective_id=2, has_side_effects=True, vmem_limit_bytes=LIMIT),
    )(counts, count_sum, toks, cots, metaz, metal, wg, wu, wd, wg2, wu2, wd2)


def whole_kernel(
    chips, nodes, locals_, tok, cot, gates, routes, wg_own, wu_own, wd_own,
    forward_home, back_home, gates_home, count_sum,
    wsem, wsend, wrecv, toks, cots, counts, metaz, metal, meta, tokz, cotl, tok_out, cot_out, count,
    send, recv, ssend, srecv, csend, crecv, wg, wu, wd, wg2, wu2, wd2, *scratch,
):
    core, ways, everyone = paths_of(nodes, locals_)
    _, twin = other_core()
    _, way = ring_way(chips)
    hail(everyone + way)
    fill_meta(gates, routes, meta)
    weights = (wg_own, wu_own, wd_own)
    load, swapped = [], []
    for index, (src, dst) in enumerate(zip(weights, (wg, wu, wd))):
        load.append(pltpu.make_async_copy(src.at[core], dst, wsem.at[index]))
        load[-1].start()
    await_all(everyone + way)

    def swap():
        for index, (src, dst) in enumerate(zip(weights, (wg2, wu2, wd2))):
            swapped.append(push(src.at[1 - core], dst, wsend.at[index], wrecv.at[index], {"dp": twin}))

    numbers, tok_copies, cot_copies, blocks = front_steps(
        nodes, locals_, ways, core, tok, cot, gates, routes, toks, cots, counts, count_sum, metaz, metal, swap,
        meta, tokz, cotl, tok_out, cot_out, count, send, recv, ssend, srecv, csend, crecv,
    )

    def received(copies):
        for copy in copies:
            copy.wait_recv()

    def ready_counts():
        received(numbers)
        count_sum[...] = jnp.sum(counts[...], axis=0)

    def ready_weights():
        for copy in load:
            copy.wait()
        received(swapped)

    main_steps(
        chips, nodes, locals_, ways, core, ready_counts, ready_weights, lambda: received(tok_copies),
        lambda: received(cot_copies), lambda: None,
        counts, count_sum, toks, cots, metaz, metal, forward_home, back_home, gates_home,
        wg, wu, wd, wg2, wu2, wd2, *scratch,
    )
    for copy in numbers + tok_copies + cot_copies + blocks + swapped:
        copy.wait_send()


def whole(chips, nodes, locals_, count, tok, cot, gates, routes, wg, wu, wd):
    rows, features = tok.shape
    top = gates.shape[0]
    hidden = wg.shape[2]
    parts = front_shapes(nodes, locals_, features, top)
    homes = main_shapes(nodes, locals_, rows, features, top)
    inner = [pltpu.VMEM(*one) for one in parts[:3] + parts[4:]]
    return pl.pallas_call(
        functools.partial(whole_kernel, chips, nodes, locals_),
        out_shape=[jax.ShapeDtypeStruct(*one) for one in homes + [parts[3]]],
        in_specs=[VMEM] * 4 + [ANY] * 3,
        out_specs=[VMEM] * 4,
        scratch_shapes=[pltpu.SemaphoreType.DMA((3,))] * 3
        + inner
        + front_scratch(nodes, locals_, rows, features, top)
        + main_scratch(chips, nodes, locals_, count, rows, features, hidden, top),
        compiler_params=pltpu.CompilerParams(collective_id=0, has_side_effects=True, vmem_limit_bytes=LIMIT),
    )(tok, cot, gates, routes, wg, wu, wd)


def total_kernel(forward, back, gates, mixed, grads, gates_out):
    mixed[...] = jnp.sum(forward[...].astype(F32), axis=0).astype(BF16)
    grads[...] = jnp.sum(back[...].astype(F32), axis=0).astype(BF16)
    gates_out[...] = jnp.sum(gates[...], axis=0)[:, : gates_out.shape[1]]


def total(forward, back, gates):
    _, rows, features = forward.shape
    half = jax.ShapeDtypeStruct((rows, features), BF16)
    return pl.pallas_call(
        total_kernel,
        out_shape=[half, half, jax.ShapeDtypeStruct((gates.shape[1], rows), F32)],
        in_specs=[VMEM] * 3,
        out_specs=[VMEM] * 3,
        compiler_params=pltpu.CompilerParams(vmem_limit_bytes=LIMIT),
    )(forward, back, gates)


def body(chips, nodes, locals_, tokens, cotangent, routes, gate_weights, w_gate, w_up, w_down):
    rows = tokens.shape[0]
    slots = nodes * locals_ * CAP
    inputs = (tokens, cotangent, gate_weights.T, routes.T, w_gate, w_up, w_down)
    *sums, count_sum = whole(chips, nodes, locals_, USUAL * chips, *inputs)

    def usual(sums, inputs):
        return total(*sums)

    def every(sums, inputs):
        toks, cots, counts, number, metaz, metal, *swapped = front(nodes, locals_, *inputs)
        weights = (*inputs[4:], *swapped)
        return total(*main(chips, nodes, locals_, slots, counts, number, toks, cots, metaz, metal, rows, *weights))

    crowded = jnp.max(count_sum[2 * locals_ :, :]) > USUAL * chips
    mixed, grads, gates = lax.cond(crowded, every, usual, tuple(sums), inputs)
    return mixed, grads, gates.T


def solution(mesh):
    chips, nodes, locals_ = mesh.shape["dp"] // 2, mesh.shape["node"], mesh.shape["local"]
    placed = (
        P(("node", "local"), "dp"),
        P(("node", "local"), "dp"),
        P(("node", "local"), None),
        P(("node", "local"), None),
        P(("node", "local"), "dp", None),
        P(("node", "local"), "dp", None),
        P(("node", "local"), None, "dp"),
    )
    return jax.shard_map(
        functools.partial(body, chips, nodes, locals_),
        mesh=mesh,
        in_specs=placed,
        out_specs=(
            P(("node", "local"), "dp"),
            P(("node", "local"), "dp"),
            P(("node", "local"), None),
        ),
        check_vma=False,
    )
```
